32 devices in a mesh: parts: 2 (over y), inner: 4 (over z), grp: 4 (over x, core).
Axes of the slice: x: 2, y: 2, z: 4, core: 2. Of those that a mesh axis runs over, the one named last changes fastest.
Arguments:
- cotangent: bfloat16 [1024, 8192], P(('parts', 'inner'), 'grp'), parts along dimension 0, may hold values from -1.5 to 1.5
- down_weight: bfloat16 [26624, 8192], P('inner', 'grp'), may hold values from -0.09375 to 0.09375
- pre_acts: bfloat16 [2, 26624, 1024], P(None, ('inner', 'grp'), 'parts'), parts along dimension 2, may hold values from -6 to 6
Outputs:
- grad_pre: bfloat16 [2, 26624, 1024], P(None, ('inner', 'grp'), 'parts'), parts along dimension 2
- grad_down: bfloat16 [53248, 8192], P(('parts', 'inner'), 'grp'), parts along dimension 0
The draws below stay inside these ranges and needn't reach their ends.
There are 2 independent parts, one for each index of `parts`. The reference program is written for one: setup_inputs(seed, part) draws one part's arguments, and reference() takes and returns one part's arrays. A program takes and returns all parts, laid end to end along the dimension named above; an argument that names none is the same for every part. Nothing has to cross between parts.
All inputs are finite; a program needn't handle non-finite values.
Results may differ from the reference program's by a relative error of at most 0.005.
Values may be sent and summed in bfloat16 or wider, within the bound.
No kernel may reach another device: no remote copies, remote signals or barrier semaphores. Data moves between devices by JAX's collectives and lax.ppermute only.
A program may use at most 192 MiB of HBM per device.

```python
import jax
import jax.numpy as jnp

D = 8192
F = 26624
TOKENS = 512


def raised(entries, own_key, source, target, blocks, factor):
    owner, partner = [(jnp.arange(entries.shape[axis_at]) // (entries.shape[axis_at] // blocks)).reshape([-1 if axis == axis_at else 1 for axis in range(entries.ndim)]) for axis_at in (source, target)]
    chosen = jax.random.permutation(own_key, blocks)[partner]
    strong = (owner == chosen) | (owner == (partner + blocks // 2) % blocks)
    return jnp.where(strong, factor * entries, entries)


def level_of(stream_key, shape, split, low, high):
    def one(axis_at, blocks):
        heights = jax.random.uniform(jax.random.fold_in(jax.random.fold_in(stream_key, 6), axis_at), (blocks,), jnp.float32, low / len(split), high / len(split))
        return jnp.repeat(jnp.exp(heights), shape[axis_at] // blocks).reshape((-1,) + (1,) * (len(shape) - axis_at - 1))

    loudness = one(*split[0])
    for cut in split[1:]:
        loudness = loudness * one(*cut)
    return loudness


def normal_values(key, dims, scale, reach, shards=(), dtype=jnp.bfloat16):
    result = scale * jax.random.normal(key, dims, jnp.float32)
    if shards:
        result = result * level_of(key, dims, shards, -0.22, 0.18)
    return jnp.clip(result, -reach, reach).astype(dtype)


def noise_with(rng, dims, deviation, reach, shards, heavy, held_as=jnp.bfloat16):
    result = deviation * jax.random.normal(rng, dims, jnp.float32)
    if shards:
        result = result * level_of(rng, dims, shards, -0.22, 0.18)
    return jnp.clip(raised(result, jax.random.fold_in(rng, 3), *heavy), -reach, reach).astype(held_as)


def setup_inputs(seed: int = 0, part: int = 0) -> dict:
    arg_keys = jax.random.split(jax.random.key(seed), 4)
    part_keys = jax.random.split(jax.random.fold_in(arg_keys[3], part), 4)
    return {
        "cotangent": normal_values(part_keys[0], (TOKENS, D), 0.25, 1.5, ((0, 4), (1, 4))),
        "down_weight": noise_with(arg_keys[1], (F, D), D ** -0.5, 0.09375, ((0, 4), (1, 4)), (1, 0, 4, 2.0)),
        "pre_acts": normal_values(part_keys[2], (2, F, TOKENS), 1.0, 6.0, ((1, 16),)),
    }


def reference(cotangent, down_weight, pre_acts):
    hidden_grad = jnp.dot(down_weight, cotangent.T, preferred_element_type=jnp.float32)
    gate = pre_acts[0].astype(jnp.float32)
    upper = pre_acts[1].astype(jnp.float32)
    sigm = jax.nn.sigmoid(gate)
    active = gate * sigm
    hidden = (active * upper).astype(jnp.bfloat16)
    grad_gate = hidden_grad * upper * sigm * (1.0 + gate * (1.0 - sigm))
    grad_upper = hidden_grad * active
    grad_pre = jnp.stack([grad_gate, grad_upper]).astype(jnp.bfloat16)
    grad_down = jnp.dot(hidden, cotangent, preferred_element_type=jnp.float32).astype(jnp.bfloat16)
    return grad_pre, grad_down
```

```python
import functools
import math

import jax
import jax.numpy as jnp
import numpy as np
from jax import lax
from jax.experimental import pallas as pl
from jax.experimental.pallas import tpu as pltpu
from jax.sharding import PartitionSpec as P

LANES = 128
MIB = 1024 * 1024


def in_vmem(array):
    return pltpu.with_memory_space_constraint(array, pltpu.VMEM), pl.BlockSpec(memory_space=pltpu.VMEM)


def in_hbm(array):
    return pltpu.with_memory_space_constraint(array, pltpu.HBM), pl.BlockSpec(memory_space=pltpu.HBM)


def anywhere(array):
    return array, pl.BlockSpec(memory_space=pl.ANY)


def sigmoid(x):
    return 0.5 * jnp.tanh(0.5 * x) + 0.5


def hidden_of(acts):
    gate = acts[0].astype(jnp.float32)
    upper = acts[1].astype(jnp.float32)
    return (gate * sigmoid(gate) * upper).astype(jnp.bfloat16)


def tile_of(rows, most):
    return max(t for t in range(16, most + 1, 16) if rows % t == 0)


TOKEN = (jax.ShapeDtypeStruct((8, LANES), jnp.float32), pl.BlockSpec((8, LANES), lambda *_: (0, 0)))


def call(kernel, name, meta, grid, ins, outs, scratch=(), alias=None, after=(), weight=1, vmem=16):
    ins = list(ins) + [anywhere(a) for a in after]
    read = len(ins) - len(after)
    aliases = {}
    if alias is not None:
        aliases = {1 + len(ins): len(outs) - 1}
        ins.append(in_hbm(alias))
    outs = list(outs) + [TOKEN]

    def body(meta_ref, *refs):
        refs = list(refs)
        token = refs.pop(len(ins) + len(outs) - 1)
        token[...] = jnp.zeros_like(token)
        kernel(meta_ref, *refs[:read], *refs[len(ins) :])

    return pl.pallas_call(
        body,
        grid_spec=pltpu.PrefetchScalarGridSpec(
            num_scalar_prefetch=1, grid=grid, in_specs=[s for _, s in ins], out_specs=[s for _, s in outs], scratch_shapes=list(scratch)
        ),
        out_shape=[s for s, _ in outs],
        input_output_aliases=aliases,
        compiler_params=pltpu.CompilerParams(vmem_limit_bytes=vmem * MIB),
        cost_estimate=pl.CostEstimate(flops=weight, bytes_accessed=1, transcendentals=0),
        name=name,
    )(meta, *[a for a, _ in ins])


def hidden_rows(acts, pieces):
    _, rows, tokens = acts.shape
    tile = math.gcd(*pieces)
    starts = [sum(pieces[:p]) for p in range(len(pieces))]

    def kernel(acts_ref, *refs):
        out_refs, (buf, sems) = refs[: len(pieces)], refs[len(pieces) :]

        def load(p):
            here = pl.ds(starts[p], pieces[p])
            return pltpu.make_async_copy(acts_ref.at[:, here, :], buf.at[:, here, :], sems.at[p])

        for p in range(len(pieces)):
            load(p).start()
        for p, ref in enumerate(out_refs):
            load(p).wait()

            @pl.loop(0, pieces[p] // tile)
            def _(i):
                at = pl.multiple_of(i * tile, tile)
                ref[pl.ds(at, tile), :] = hidden_of(buf[:, pl.ds(starts[p] + at, tile), :])

    array, spec = in_hbm(acts)
    return pl.pallas_call(
        kernel,
        in_specs=[spec],
        out_specs=[pl.BlockSpec(memory_space=pltpu.VMEM)] * len(pieces),
        out_shape=[pltpu.VMEM((n, tokens), acts.dtype) for n in pieces],
        scratch_shapes=[pltpu.VMEM(acts.shape, acts.dtype), pltpu.SemaphoreType.DMA((len(pieces),))],
        compiler_params=pltpu.CompilerParams(vmem_limit_bytes=12 * MIB),
        cost_estimate=pl.CostEstimate(flops=1, bytes_accessed=1, transcendentals=0),
        name="hidden",
    )(array)


class Slot:
    def __init__(self, number, blocks):
        self.number, self.blocks = number, blocks

    def start(self, meta_ref, refs, target, sem):
        offset = meta_ref[1 + self.number] - meta_ref[1]
        for key, ref in zip(self.blocks, refs, strict=True):

            @pl.when(offset == key)
            def _():
                pltpu.make_async_copy(ref, target, sem).start()

    def wait(self, refs, target, sem):
        pltpu.make_async_copy(refs[0], target, sem).wait()


def fetch(slots, meta_ref, refs, targets, sems):
    waits = []
    for n, slot in enumerate(slots):
        mine, refs = refs[: len(slot.blocks)], refs[len(slot.blocks) :]
        slot.start(meta_ref, mine, targets[n], sems.at[n])
        waits.append(functools.partial(slot.wait, mine, targets[n], sems.at[n]))
    return lambda: [wait() for wait in waits]


def blocks_of(slots):
    return [(block, pl.BlockSpec(memory_space=pl.ANY)) for slot in slots for block in slot.blocks.values()]


def clamped(first, steps):
    return lambda k: jnp.clip(k - first, 0, steps - 1)


def partials(meta, masks, weight, rows, tokens, dtypes, splits, slots=None, turned=None, adds=None, after=()):
    feats = weight.shape[1]
    tile = rows // 4
    steps = rows // tile
    total = len(masks) * steps
    blocks = blocks_of(slots) if slots else [in_vmem(turned)]
    each = tokens // len(slots) if slots else 0
    extra = [a for group in adds or [] for a in group]
    per = len(extra) // len(masks)

    def kernel(meta_ref, w_ref, *refs):
        block_refs, refs = refs[: len(blocks)], refs[len(blocks) :]
        add_refs, refs = refs[: len(extra)], refs[len(extra) :]
        out_refs, refs = refs[: len(masks) * splits], refs[len(masks) * splits :]
        if slots:
            turned_ref, buf, w_sems, rows_buf, sems = refs
        else:
            turned_ref, (buf, w_sems) = block_refs[0], refs
        k = pl.program_id(0)

        def copy(step):
            block = meta_ref[0] ^ masks[step // steps]
            at = pl.multiple_of(block * rows + step % steps * tile, tile)
            return pltpu.make_async_copy(w_ref.at[pl.ds(at, tile), :], buf.at[pl.ds(step * tile, tile), :], w_sems.at[step])

        @pl.when(k == 0)
        def _():
            if slots:
                targets = [rows_buf.at[pl.ds(n * each, each), :] for n in range(len(slots))]
                wait = fetch(slots, meta_ref, block_refs, targets, sems)
            for step in range(total):
                copy(step).start()
            if slots:
                wait()
                turned_ref[...] = rows_buf[...].T

        for step in range(total):

            @pl.when(k == step)
            def _():
                copy(step).wait()

        w = buf[pl.ds(pl.multiple_of(k * tile, tile), tile), :]
        out = jnp.dot(w, turned_ref[...], preferred_element_type=jnp.float32)
        for step in range(total):
            j, i = step // steps, step % steps

            @pl.when(k == step)
            def _():
                value = out
                if extra:
                    value = value + add_refs[j * per + i * per // steps][...].astype(jnp.float32)
                out_refs[j * splits + i * splits // steps][...] = value.astype(dtypes[j])

    def spec(j, p, count):
        index = clamped(j * steps + p * steps // count, steps // count)
        return pl.BlockSpec((tile, tokens), lambda k, m: (index(k), 0))

    ins = [in_hbm(weight), *blocks]
    ins += [(piece, spec(n // per, n % per, per)) for n, piece in enumerate(extra)]
    outs = [
        (jax.ShapeDtypeStruct((rows // splits, tokens), dtype), spec(j, p, splits)) for j, dtype in enumerate(dtypes) for p in range(splits)
    ]
    scratch = [pltpu.VMEM((total * tile, feats), weight.dtype), pltpu.SemaphoreType.DMA((total,))]
    if slots:
        outs.append((pltpu.VMEM((feats, tokens), weight.dtype), pl.BlockSpec(memory_space=pltpu.VMEM)))
        scratch += [pltpu.VMEM((tokens, feats), weight.dtype), pltpu.SemaphoreType.DMA((len(slots),))]
    return call(kernel, "partials", meta, (total,), ins, outs, scratch, after=after, vmem=24)


def all_slots(meta, slots, each, feats, after=()):
    blocks = blocks_of(slots)

    def kernel(meta_ref, *refs):
        block_refs, (out_ref, sems) = refs[: len(blocks)], refs[len(blocks) :]
        starts = [pl.multiple_of(meta_ref[1 + slot.number] * each, each) for slot in slots]
        fetch(slots, meta_ref, block_refs, [out_ref.at[pl.ds(at, each), :] for at in starts], sems)()

    shape = pltpu.VMEM((len(slots) * each, feats), jnp.bfloat16)
    outs = [(shape, pl.BlockSpec(memory_space=pltpu.VMEM))]
    return call(kernel, "token_rows", meta, (1,), blocks, outs, [pltpu.SemaphoreType.DMA((len(slots),))], after=after, vmem=4)


def weight_grad(meta, masks, hiddens, cots, out, total_rows, after=(), weight=1):
    tokens, feats = cots.shape
    sizes = [p.shape[0] for p in hiddens[0]]
    rows = sum(sizes)
    tile = rows // 2
    steps = rows // tile
    flat = [p for pieces in hiddens for p in pieces]

    def kernel(meta_ref, cot_ref, *refs):
        piece_refs, (out_ref,) = refs[: len(flat)], refs[len(flat) :]
        for step in range(len(masks) * steps):

            @pl.when(pl.program_id(0) == step)
            def _():
                j, low = step // steps, step % steps * tile
                parts, at = [], 0
                for p, size in enumerate(sizes):
                    first, last = max(low, at), min(low + tile, at + size)
                    if first < last:
                        parts.append(piece_refs[j * len(sizes) + p][first - at : last - at, :])
                    at += size
                h = parts[0] if len(parts) == 1 else jnp.concatenate(parts)
                out_ref[...] = jnp.dot(h, cot_ref[...], preferred_element_type=jnp.float32).astype(out_ref.dtype)

    def place(k, m):
        block = m[0] ^ masks[0]
        for j in range(1, len(masks)):
            block = jnp.where(k // steps == j, m[0] ^ masks[j], block)
        return block * steps + k % steps, 0

    return call(
        kernel, "weight_grad", meta, (len(masks) * steps,),
        [in_vmem(cots), *[in_vmem(p) for p in flat]],
        [(jax.ShapeDtypeStruct((total_rows, feats), cots.dtype), pl.BlockSpec((tile, feats), place))],
        alias=out, after=after, weight=weight, vmem=18,
    )


def gate_grad(meta, first, start, acts, own, far, out, after=()):
    rows, tokens = far.shape
    tile = rows // 4

    def kernel(meta_ref, acts_ref, own_ref, far_ref, out_ref):
        i, j = pl.program_id(0), pl.program_id(1)
        columns = pl.ds(pl.multiple_of(meta_ref[1 + first + j] * LANES, LANES), LANES)
        lanes = pl.ds(pl.multiple_of(j * LANES, LANES), LANES)
        here = pl.ds(pl.multiple_of(i * tile, tile), tile)
        there = pl.ds(pl.multiple_of(start + i * tile, tile), tile)
        grad = own_ref[here, lanes] + far_ref[here, lanes].astype(jnp.float32)
        gate = acts_ref[0, there, columns].astype(jnp.float32)
        upper = acts_ref[1, there, columns].astype(jnp.float32)
        sigm = sigmoid(gate)
        out_ref[0] = (grad * upper * sigm * (1.0 + gate * (1.0 - sigm))).astype(out_ref.dtype)
        out_ref[1] = (grad * (gate * sigm)).astype(out_ref.dtype)

    spec = pl.BlockSpec((2, tile, LANES), lambda i, j, m: (0, start // tile + i, m[1 + first + j]))
    return call(
        kernel, "gate_grad", meta, (rows // tile, tokens // LANES),
        [in_vmem(acts), in_vmem(own), in_vmem(far)],
        [(jax.ShapeDtypeStruct(acts.shape, acts.dtype), spec)],
        alias=out, after=after, vmem=6,
    )


def arrivals(size):
    return [sorted((k for k in range(size) if k != z), key=lambda k: (abs(k - z), (k - z) * (1 if z % 2 else -1))) for z in range(size)]


def along(block, axis, size, step, first=0):
    left = lax.ppermute(block[0], axis, [(k, k + step) for k in range(first, size - step)])
    right = lax.ppermute(block[1], axis, [(k + step, k) for k in range(size - step - first)])
    return left, right


def slot_of(got, s, size):
    order = arrivals(size)
    offsets = {order[k][s - 1] - k for k in range(size)}
    return Slot(s, {offset: got[offset] for offset in sorted(offsets)})


def describe(me, z, size):
    order = arrivals(size)
    tables = [np.array([0, k, *order[k]], np.int32) for k in range(size)]
    meta = jnp.asarray(tables[0])
    for k in range(1, size):
        meta = jnp.where(z == k, tables[k], meta)
    return meta + me * np.array([1] + [0] * size, np.int32)


def two_level(inner, cotangent, down_weight, pre_acts):
    me, z = lax.axis_index("grp"), lax.axis_index("inner")
    total_rows = down_weight.shape[0]
    rows = pre_acts.shape[1]
    across_core = functools.partial(lax.ppermute, axis_name="grp", perm=[(k, k ^ 1) for k in range(4)])
    across_x = functools.partial(lax.ppermute, axis_name="grp", perm=[(k, k ^ 2) for k in range(4)])
    meta = describe(me, z, inner)
    bf16, f32 = jnp.bfloat16, jnp.float32

    unit = rows // 26
    hidden = hidden_rows(pre_acts, (12 * unit, 7 * unit, 7 * unit))
    hidden, cotangent = lax.optimization_barrier((hidden, cotangent))
    hidden_far = [across_x(h) for h in hidden]

    each, feats = cotangent.shape
    got = {}
    pair = (cotangent, cotangent)
    for step in range(1, inner):
        pair = along(pair, "inner", inner, 1, step - 1)
        got[-step], got[step] = pair
    slots = [Slot(0, {0: cotangent})] + [slot_of(got, s, inner) for s in range(1, inner)]
    hidden_core = [across_core(h) for h in hidden]

    half = inner // 2
    tokens = half * each

    *sent, turned, _ = partials(meta, (3, 1), down_weight, rows, tokens, (bf16, bf16), 2, slots[:half], after=(hidden_far[0],))
    back = [across_core(p) for p in sent]
    a_sum, a_own, done = partials(
        meta, (2, 0), down_weight, rows, tokens, (bf16, f32), 1, turned=turned, adds=(back[:2], back[2:]), after=(hidden_far[1],)
    )
    a_far = across_x(a_sum)

    *sent, turned, done = partials(
        meta, (3, 1), down_weight, rows, tokens, (bf16, bf16), 2, slots[half:], after=(done, hidden_far[2])
    )
    back = [across_core(p) for p in sent]
    cots, done = all_slots(meta, slots, each, feats, after=(done,))
    b_sum0, b_sum1, b_own0, b_own1, done = partials(
        meta, (2, 0), down_weight, rows, tokens, (bf16, f32), 2, turned=turned, adds=(back[:2], back[2:]), after=(done,)
    )
    b_far0, b_far1 = across_x(b_sum0), across_x(b_sum1)
    hidden_both = [across_core(h) for h in hidden_far]

    grad_down, done = weight_grad(meta, (0, 1), (hidden, hidden_core), cots, None, total_rows, after=(done,))
    grad_pre, done = gate_grad(meta, 0, 0, pre_acts, a_own, a_far, None, after=(done,))
    grad_down, done = weight_grad(
        meta, (2, 3), (hidden_far, hidden_both), cots, grad_down, total_rows, after=(done,), weight=100 * 10**9
    )
    grad_pre, done = gate_grad(meta, half, 0, pre_acts, b_own0, b_far0, grad_pre, after=(done,))
    grad_pre, _ = gate_grad(meta, half, rows // 2, pre_acts, b_own1, b_far1, grad_pre, after=(done,))
    return grad_pre, grad_down


def plain(cotangent, down_weight, pre_acts):
    all_rows = lax.all_gather(cotangent, "inner", axis=0, tiled=True)
    hidden = hidden_of(pre_acts)
    grad = lax.psum_scatter(
        jnp.einsum("fd,td->ft", down_weight, all_rows, preferred_element_type=jnp.float32),
        "grp",
        scatter_dimension=0,
        tiled=True,
    )
    gate = pre_acts[0].astype(jnp.float32)
    upper = pre_acts[1].astype(jnp.float32)
    sigm = jax.nn.sigmoid(gate)
    grad_gate = grad * upper * sigm * (1.0 + gate * (1.0 - sigm))
    grad_pre = jnp.stack([grad_gate, grad * (gate * sigm)]).astype(jnp.bfloat16)
    grad_down = jnp.dot(
        lax.all_gather(hidden, "grp", axis=0, tiled=True), all_rows, preferred_element_type=jnp.float32
    ).astype(jnp.bfloat16)
    return grad_pre, grad_down


def solution(mesh):
    inner, grp = mesh.shape["inner"], mesh.shape["grp"]

    def on_device(cotangent, down_weight, pre_acts):
        if grp == 4 and inner % 2 == 0 and cotangent.shape[0] == LANES:
            return two_level(inner, cotangent, down_weight, pre_acts)
        return plain(cotangent, down_weight, pre_acts)

    return jax.shard_map(
        on_device,
        mesh=mesh,
        in_specs=(
            P(("parts", "inner"), "grp"),
            P("inner", "grp"),
            P(None, ("inner", "grp"), "parts"),
        ),
        out_specs=(P(None, ("inner", "grp"), "parts"), P(("parts", "inner"), "grp")),
        check_vma=False,
    )
```

```python
import functools
import math

import jax
import jax.numpy as jnp
import numpy as np
from jax import lax
from jax.experimental import pallas as pl
from jax.experimental.pallas import tpu as pltpu
from jax.sharding import PartitionSpec as P

LANES = 128
LONG, SHORT, MIDDLE, BRIEF = 20 * 10**9, 4700 * 10**6, 4190 * 10**6, 790 * 10**6
MIB = 1024 * 1024


def in_vmem(array):
    return pltpu.with_memory_space_constraint(array, pltpu.VMEM), pl.BlockSpec(memory_space=pltpu.VMEM)


def in_hbm(array):
    return pltpu.with_memory_space_constraint(array, pltpu.HBM), pl.BlockSpec(memory_space=pltpu.HBM)


def anywhere(array):
    return array, pl.BlockSpec(memory_space=pl.ANY)


def sigmoid(x):
    return 0.5 * jnp.tanh(0.5 * x) + 0.5


def hidden_of(acts):
    gate = acts[0].astype(jnp.float32)
    upper = acts[1].astype(jnp.float32)
    return (gate * sigmoid(gate) * upper).astype(jnp.bfloat16)


def tile_of(rows, most):
    return max(t for t in range(16, most + 1, 16) if rows % t == 0)


TOKEN = (pltpu.VMEM((8, LANES), jnp.float32), pl.BlockSpec(memory_space=pltpu.VMEM))


def call(kernel, name, meta, grid, ins, outs, scratch=(), alias=None, after=(), weight=1, vmem=16):
    ins = list(ins) + [anywhere(a) for a in after]
    read = len(ins) - len(after)
    aliases = {}
    if alias is not None:
        aliases = {1 + len(ins): len(outs) - 1}
        ins.append(in_hbm(alias))
    outs = list(outs) + [TOKEN]

    def body(meta_ref, *refs):
        refs = list(refs)
        token = refs.pop(len(ins) + len(outs) - 1)
        token[...] = jnp.zeros_like(token)
        kernel(meta_ref, *refs[:read], *refs[len(ins) :])

    return pl.pallas_call(
        body,
        grid_spec=pltpu.PrefetchScalarGridSpec(
            num_scalar_prefetch=1, grid=grid, in_specs=[s for _, s in ins], out_specs=[s for _, s in outs], scratch_shapes=list(scratch)
        ),
        out_shape=[s for s, _ in outs],
        input_output_aliases=aliases,
        compiler_params=pltpu.CompilerParams(vmem_limit_bytes=vmem * MIB),
        cost_estimate=pl.CostEstimate(flops=weight, bytes_accessed=1, transcendentals=0),
        name=name,
    )(meta, *[a for a, _ in ins])


def hidden_rows(acts, start, pieces, after=()):
    _, _, tokens = acts.shape
    rows = sum(pieces)
    tile = math.gcd(*pieces)
    starts = [sum(pieces[:p]) for p in range(len(pieces))]

    def kernel(acts_ref, *refs):
        refs = refs[len(after) :]
        out_refs, (buf, sems) = refs[: len(pieces)], refs[len(pieces) :]

        def load(p):
            there, here = pl.ds(start + starts[p], pieces[p]), pl.ds(starts[p], pieces[p])
            return pltpu.make_async_copy(acts_ref.at[:, there, :], buf.at[:, here, :], sems.at[p])

        for p in range(len(pieces)):
            load(p).start()
        for p, ref in enumerate(out_refs):
            load(p).wait()
            for at in range(0, pieces[p], tile // 4):
                ref[pl.ds(at, tile // 4), :] = hidden_of(buf[:, pl.ds(starts[p] + at, tile // 4), :])

    array, spec = in_hbm(acts)
    return pl.pallas_call(
        kernel,
        in_specs=[spec, *[anywhere(a)[1] for a in after]],
        out_specs=[pl.BlockSpec(memory_space=pltpu.VMEM)] * len(pieces),
        out_shape=[pltpu.VMEM((n, tokens), acts.dtype) for n in pieces],
        scratch_shapes=[pltpu.VMEM((2, rows, tokens), acts.dtype), pltpu.SemaphoreType.DMA((len(pieces),))],
        compiler_params=pltpu.CompilerParams(vmem_limit_bytes=8 * MIB),
        cost_estimate=pl.CostEstimate(flops=1, bytes_accessed=1, transcendentals=0),
        name="hidden",
    )(array, *after)


class Slot:
    def __init__(self, number, blocks, places):
        self.number, self.blocks, self.places = number, blocks, places

    def start(self, meta_ref, refs, target, sem):
        for ref, places in zip(refs, self.places, strict=True):

            @pl.when(functools.reduce(jnp.logical_or, [meta_ref[1] == z for z in places]))
            def _():
                pltpu.make_async_copy(ref, target, sem).start()

    def wait(self, refs, target, sem):
        pltpu.make_async_copy(refs[0], target, sem).wait()


def fetch(slots, meta_ref, refs, targets, sems):
    waits = []
    for n, slot in enumerate(slots):
        mine, refs = refs[: len(slot.blocks)], refs[len(slot.blocks) :]
        slot.start(meta_ref, mine, targets[n], sems.at[n])
        waits.append(functools.partial(slot.wait, mine, targets[n], sems.at[n]))
    return lambda: [wait() for wait in waits]


def blocks_of(slots):
    return [anywhere(block) for slot in slots for block in slot.blocks]


def partials(meta, masks, weight, rows, tokens, dtypes, splits, slots=None, turned=None, adds=None, keep=True, after=(), weight_of=1):
    feats = weight.shape[1]
    tile = rows // (4 if keep else 2)
    steps = rows // tile
    total = len(masks) * steps
    depth = 3
    blocks = blocks_of(slots) if slots else [in_vmem(turned)]
    each = tokens // len(slots) if slots else 0
    extra = [a for group in adds or [] for a in group]
    per = len(extra) // len(masks)

    def kernel(meta_ref, w_ref, *refs):
        block_refs, refs = refs[: len(blocks)], refs[len(blocks) :]
        add_refs, refs = refs[: len(extra)], refs[len(extra) :]
        out_refs, refs = refs[: len(masks) * splits], list(refs[len(masks) * splits :])
        turned_ref = refs.pop(0) if slots else block_refs[0]
        kept_ref = refs.pop(0) if keep else w_ref
        k = pl.program_id(0)

        def copy(step):
            block = meta_ref[0] ^ masks[step // steps]
            at = pl.multiple_of(block * rows + step % steps * tile, tile)
            return pltpu.make_async_copy(w_ref.at[pl.ds(at, tile), :], kept_ref.at[pl.ds(step * tile, tile), :], refs[0].at[step])

        @pl.when(k == 0)
        def _():
            if slots:
                rows_buf, sems = refs[-2:]
                targets = [rows_buf.at[pl.ds(n * each, each), :] for n in range(len(slots))]
                wait = fetch(slots, meta_ref, block_refs, targets, sems)
            if keep:
                for step in range(depth - 1):
                    copy(step).start()
            if slots:
                wait()
                turned_ref[...] = rows_buf[...].T

        if keep:
            for step in range(total):

                @pl.when(k == step)
                def _():
                    if step + depth - 1 < total:
                        copy(step + depth - 1).start()
                    copy(step).wait()

        w = kept_ref[pl.ds(pl.multiple_of(k * tile, tile), tile), :]
        out = jnp.dot(w, turned_ref[...], preferred_element_type=jnp.float32)
        for step in range(total):
            j, i = step // steps, step % steps

            @pl.when(k == step)
            def _():
                value = out
                if extra:
                    add_ref, at = add_refs[j * per + i * per // steps], i % (steps // per) * tile
                    value = value + add_ref[at : at + tile, :].astype(jnp.float32)
                at = i % (steps // splits) * tile
                out_refs[j * splits + i * splits // steps][at : at + tile, :] = value.astype(dtypes[j])

    in_place = pl.BlockSpec(memory_space=pltpu.VMEM)
    ins = [in_hbm(weight) if keep else in_vmem(weight), *blocks, *[in_vmem(piece) for piece in extra]]
    outs = [(pltpu.VMEM((rows // splits, tokens), dtype), in_place) for dtype in dtypes for _ in range(splits)]
    scratch = []
    if slots:
        outs.append((pltpu.VMEM((feats, tokens), weight.dtype), in_place))
        scratch = [pltpu.VMEM((tokens, feats), weight.dtype), pltpu.SemaphoreType.DMA((len(slots),))]
    if keep:
        outs.append((pltpu.VMEM((total * tile, feats), weight.dtype), in_place))
        scratch = [pltpu.SemaphoreType.DMA((total,)), *scratch]
    return call(kernel, "partials", meta, (total,), ins, outs, scratch, after=after, weight=weight_of, vmem=8)


def turned_slots(meta, slots, each, feats, after=(), weight=1):
    blocks = blocks_of(slots)
    tokens = len(slots) * each

    def kernel(meta_ref, *refs):
        block_refs, (out_ref, buf, sems) = refs[: len(blocks)], refs[len(blocks) :]
        fetch(slots, meta_ref, block_refs, [buf.at[pl.ds(n * each, each), :] for n in range(len(slots))], sems)()
        out_ref[...] = buf[...].T

    outs = [(pltpu.VMEM((feats, tokens), jnp.bfloat16), pl.BlockSpec(memory_space=pltpu.VMEM))]
    scratch = [pltpu.VMEM((tokens, feats), jnp.bfloat16), pltpu.SemaphoreType.DMA((len(slots),))]
    return call(kernel, "turned", meta, (1,), blocks, outs, scratch, after=after, weight=weight, vmem=6)


def all_slots(meta, slots, each, feats, after=()):
    blocks = blocks_of(slots)

    def kernel(meta_ref, *refs):
        block_refs, (out_ref, sems) = refs[: len(blocks)], refs[len(blocks) :]
        starts = [pl.multiple_of(meta_ref[1 + slot.number] * each, each) for slot in slots]
        fetch(slots, meta_ref, block_refs, [out_ref.at[pl.ds(at, each), :] for at in starts], sems)()

    shape = pltpu.VMEM((len(slots) * each, feats), jnp.bfloat16)
    outs = [(shape, pl.BlockSpec(memory_space=pltpu.VMEM))]
    return call(kernel, "token_rows", meta, (1,), blocks, outs, [pltpu.SemaphoreType.DMA((len(slots),))], after=after, vmem=4)


def weight_grad(meta, masks, hiddens, cots, out, total_rows, after=(), weight=1):
    tokens, feats = cots.shape
    steps = len(hiddens[0])
    tile = hiddens[0][0].shape[0]
    flat = [p for pieces in hiddens for p in pieces]

    def kernel(meta_ref, cot_ref, *refs):
        piece_refs, (out_ref, buf, sems) = refs[: len(flat)], refs[len(flat) :]
        k = pl.program_id(0)

        def copy(step):
            return pltpu.make_async_copy(piece_refs[step], buf.at[step % 2], sems.at[step % 2])

        @pl.when(k == 0)
        def _():
            copy(0).start()

        for step in range(len(flat)):

            @pl.when(k == step)
            def _():
                copy(step).wait()
                if step + 1 < len(flat):
                    copy(step + 1).start()

        out_ref[...] = jnp.dot(buf[lax.rem(k, 2)], cot_ref[...], preferred_element_type=jnp.float32).astype(out_ref.dtype)

    def place(k, m):
        block = m[0] ^ masks[0]
        for j in range(1, len(masks)):
            block = jnp.where(k // steps == j, m[0] ^ masks[j], block)
        return block * steps + k % steps, 0

    return call(
        kernel, "weight_grad", meta, (len(flat),),
        [in_vmem(cots), *[anywhere(p) for p in flat]],
        [(jax.ShapeDtypeStruct((total_rows, feats), cots.dtype), pl.BlockSpec((tile, feats), place))],
        [pltpu.VMEM((2, tile, tokens), cots.dtype), pltpu.SemaphoreType.DMA((2,))],
        alias=out, after=after, weight=weight, vmem=20,
    )


def gate_grad(meta, acts, early, weight, turned, back, far, after=()):
    _, rows, tokens = acts.shape
    feats, half = turned.shape
    tile = rows // 4
    per = len(back)

    def kernel(meta_ref, acts_ref, mine_ref, theirs_ref, w_ref, turned_ref, *refs):
        back_refs, far_ref, out_ref = refs[:per], refs[per], refs[per + 1]
        i = pl.program_id(0)
        here = pl.ds(pl.multiple_of(i * tile, tile), tile)
        late = jnp.dot(w_ref[here, :], turned_ref[...], preferred_element_type=jnp.float32)
        late = late + far_ref[here, :].astype(jnp.float32)
        there = pl.ds(pl.multiple_of(i % (4 // per) * tile, tile), tile)
        added = back_refs[0][there, :]
        for p in range(1, per):
            added = jnp.where(i * per // 4 == p, back_refs[p][there, :], added)
        late = late + added.astype(jnp.float32)
        for slot in range(tokens // LANES):
            lanes = slice(slot * LANES % half, slot * LANES % half + LANES)
            if slot * LANES < half:
                grad = mine_ref[here, lanes] + theirs_ref[here, lanes].astype(jnp.float32)
            else:
                grad = late[:, lanes]
            columns = pl.ds(pl.multiple_of(meta_ref[1 + slot] * LANES, LANES), LANES)
            gate = acts_ref[0, here, columns].astype(jnp.float32)
            upper = acts_ref[1, here, columns].astype(jnp.float32)
            sigm = sigmoid(gate)
            out_ref[0, :, columns] = (grad * upper * sigm * (1.0 + gate * (1.0 - sigm))).astype(out_ref.dtype)
            out_ref[1, :, columns] = (grad * (gate * sigm)).astype(out_ref.dtype)

    ins = [in_vmem(a) for a in (acts, *early, weight, turned, *back, far)]
    outs = [(jax.ShapeDtypeStruct(acts.shape, acts.dtype), pl.BlockSpec((2, tile, tokens), lambda i, m: (0, i, 0)))]
    return call(kernel, "gate_grad", meta, (4,), ins, outs, after=after, vmem=12)


def wait_for(meta, after, weight):
    return call(lambda meta_ref: None, "arrived", meta, (1,), [], [], after=after, weight=weight, vmem=1)[0]


ARRIVALS = ((0, 1, 2, 3), (1, 0, 2, 3), (2, 3, 1, 0), (3, 2, 1, 0))


def describe(me, z):
    tables = [np.array([0, *order], np.int32) for order in ARRIVALS]
    meta = jnp.asarray(tables[0])
    for k in range(1, len(tables)):
        meta = jnp.where(z == k, tables[k], meta)
    return meta + me * np.array([1, 0, 0, 0, 0], np.int32)


def two_level(cotangent, down_weight, pre_acts):
    me, z = lax.axis_index("grp"), lax.axis_index("inner")
    total_rows = down_weight.shape[0]
    rows = pre_acts.shape[1]
    each, feats = cotangent.shape
    tokens = 2 * each
    across_core = functools.partial(lax.ppermute, axis_name="grp", perm=[(k, k ^ 1) for k in range(4)])
    across_x = functools.partial(lax.ppermute, axis_name="grp", perm=[(k, k ^ 2) for k in range(4)])
    in_pairs = functools.partial(lax.ppermute, axis_name="inner", perm=[(0, 1), (1, 0), (2, 3), (3, 2)])
    in_middle = functools.partial(lax.ppermute, axis_name="inner", perm=[(1, 2), (2, 1)])
    outwards = functools.partial(lax.ppermute, axis_name="inner", perm=[(1, 0), (2, 3)])
    meta = describe(me, z)
    bf16, f32 = jnp.bfloat16, jnp.float32

    hidden = hidden_rows(pre_acts, 0, (rows // 2,))
    hidden = [*hidden, *hidden_rows(pre_acts, rows // 2, (rows // 2,), after=hidden)]
    hidden[1], cotangent = lax.optimization_barrier((hidden[1], cotangent))
    hidden_far = [across_x(h) for h in hidden]
    hidden_core = [across_core(h) for h in hidden]

    near, second = in_pairs(cotangent), in_middle(cotangent)
    third, outer = in_middle(near), outwards(second)
    third, outer = lax.optimization_barrier((third, outer))
    outmost = outwards(third)
    slots = [
        Slot(0, [cotangent], [(0, 1, 2, 3)]),
        Slot(1, [near], [(0, 1, 2, 3)]),
        Slot(2, [second, outer], [(1, 2), (0, 3)]),
        Slot(3, [third, outmost], [(1, 2), (0, 3)]),
    ]

    sums = functools.partial(partials, meta, rows=rows, tokens=tokens)
    turned, done = turned_slots(meta, slots[:2], each, feats, after=(hidden_far[0],), weight=SHORT)
    *sent, kept_sent, _ = sums(
        (3, 1), down_weight, dtypes=(bf16, bf16), splits=2, turned=turned, after=(done, *hidden_core), weight_of=LONG
    )
    back = [across_core(p) for p in sent]
    a_sum, kept_sum, done = sums((2,), down_weight, dtypes=(bf16,), splits=1, turned=turned, adds=(back[:2],))
    a_far = across_x(a_sum)
    a_own, kept_own, done = sums(
        (0,), down_weight, dtypes=(f32,), splits=1, turned=turned, adds=(back[2:],), after=(done, hidden_far[1]), weight_of=MIDDLE
    )

    *sent, turned, done = sums((3, 1), kept_sent, dtypes=(bf16, bf16), splits=2, slots=slots[2:], keep=False, after=(done,))
    back = [across_core(p) for p in sent]
    cots, done = all_slots(meta, slots, each, feats, after=(done,))
    hidden_both = [across_core(h) for h in hidden_far]
    b_sum, done = sums((2,), kept_sum, dtypes=(bf16,), splits=1, turned=turned, adds=(back[:2],), keep=False, after=(done,))
    b_far = across_x(b_sum)
    done = wait_for(meta, (done, a_far), BRIEF)
    grad_down, done = weight_grad(
        meta, (0, 1, 2, 3), (hidden, hidden_core, hidden_far, hidden_both), cots, None, total_rows, after=(done,), weight=200 * 10**9
    )
    grad_pre, _ = gate_grad(meta, pre_acts, (a_own, a_far), kept_own, turned, back[2:], b_far, after=(done,))
    return grad_pre, grad_down


def plain(cotangent, down_weight, pre_acts):
    all_rows = lax.all_gather(cotangent, "inner", axis=0, tiled=True)
    hidden = hidden_of(pre_acts)
    grad = lax.psum_scatter(
        jnp.einsum("fd,td->ft", down_weight, all_rows, preferred_element_type=jnp.float32),
        "grp",
        scatter_dimension=0,
        tiled=True,
    )
    gate = pre_acts[0].astype(jnp.float32)
    upper = pre_acts[1].astype(jnp.float32)
    sigm = jax.nn.sigmoid(gate)
    grad_gate = grad * upper * sigm * (1.0 + gate * (1.0 - sigm))
    grad_pre = jnp.stack([grad_gate, grad * (gate * sigm)]).astype(jnp.bfloat16)
    grad_down = jnp.dot(
        lax.all_gather(hidden, "grp", axis=0, tiled=True), all_rows, preferred_element_type=jnp.float32
    ).astype(jnp.bfloat16)
    return grad_pre, grad_down


def solution(mesh):
    inner, grp = mesh.shape["inner"], mesh.shape["grp"]

    def on_device(cotangent, down_weight, pre_acts):
        if grp == 4 and inner == 4 and cotangent.shape[0] == LANES and pre_acts.shape[1] % 128 == 0:
            return two_level(cotangent, down_weight, pre_acts)
        return plain(cotangent, down_weight, pre_acts)

    return jax.shard_map(
        on_device,
        mesh=mesh,
        in_specs=(
            P(("parts", "inner"), "grp"),
            P("inner", "grp"),
            P(None, ("inner", "grp"), "parts"),
        ),
        out_specs=(P(None, ("inner", "grp"), "parts"), P(("parts", "inner"), "grp")),
        check_vma=False,
    )
```

```python
import functools
import math

import jax
import jax.numpy as jnp
import numpy as np
from jax import lax
from jax.experimental import pallas as pl
from jax.experimental.pallas import tpu as pltpu
from jax.sharding import PartitionSpec as P

LANES = 128
TURNED, ARRIVED = 7000 * 10**6, 9200 * 10**6
MIB = 1024 * 1024


def in_vmem(array):
    return pltpu.with_memory_space_constraint(array, pltpu.VMEM), pl.BlockSpec(memory_space=pltpu.VMEM)


def in_hbm(array):
    return pltpu.with_memory_space_constraint(array, pltpu.HBM), pl.BlockSpec(memory_space=pltpu.HBM)


def anywhere(array):
    return array, pl.BlockSpec(memory_space=pl.ANY)


def sigmoid(x):
    return 0.5 * jnp.tanh(0.5 * x) + 0.5


def hidden_of(acts):
    gate = acts[0].astype(jnp.float32)
    upper = acts[1].astype(jnp.float32)
    return (gate * sigmoid(gate) * upper).astype(jnp.bfloat16)


def tile_of(rows, most):
    return max(t for t in range(16, most + 1, 16) if rows % t == 0)


TOKEN = (pltpu.VMEM((8, LANES), jnp.float32), pl.BlockSpec(memory_space=pltpu.VMEM))


def call(kernel, name, meta, grid, ins, outs, scratch=(), alias=None, after=(), weight=1, vmem=16):
    ins = list(ins) + [anywhere(a) for a in after]
    read = len(ins) - len(after)
    aliases = {}
    if alias is not None:
        aliases = {1 + len(ins): len(outs) - 1}
        ins.append(in_hbm(alias))
    outs = list(outs) + [TOKEN]

    def body(meta_ref, *refs):
        refs = list(refs)
        token = refs.pop(len(ins) + len(outs) - 1)
        token[...] = jnp.zeros_like(token)
        kernel(meta_ref, *refs[:read], *refs[len(ins) :])

    return pl.pallas_call(
        body,
        grid_spec=pltpu.PrefetchScalarGridSpec(
            num_scalar_prefetch=1, grid=grid, in_specs=[s for _, s in ins], out_specs=[s for _, s in outs], scratch_shapes=list(scratch)
        ),
        out_shape=[s for s, _ in outs],
        input_output_aliases=aliases,
        compiler_params=pltpu.CompilerParams(vmem_limit_bytes=vmem * MIB),
        cost_estimate=pl.CostEstimate(flops=weight, bytes_accessed=1, transcendentals=0),
        name=name,
    )(meta, *[a for a, _ in ins])


def hidden_rows(acts):
    _, rows, tokens = acts.shape
    parts = 4
    tile = rows // parts

    def kernel(acts_ref, out_ref, buf, sems):
        def load(p):
            here = pl.ds(p * tile, tile)
            return pltpu.make_async_copy(acts_ref.at[:, here, :], buf.at[:, here, :], sems.at[p])

        for p in range(2):
            load(p).start()
        for p in range(parts):
            load(p).wait()
            if p + 2 < parts:
                load(p + 2).start()
            for at in range(p * tile, (p + 1) * tile, tile // 2):
                out_ref[pl.ds(at, tile // 2), :] = hidden_of(buf[:, pl.ds(at, tile // 2), :])

    array, spec = in_hbm(acts)
    return pl.pallas_call(
        kernel,
        in_specs=[spec],
        out_specs=pl.BlockSpec(memory_space=pltpu.VMEM),
        out_shape=pltpu.VMEM((rows, tokens), acts.dtype),
        scratch_shapes=[pltpu.VMEM(acts.shape, acts.dtype), pltpu.SemaphoreType.DMA((parts,))],
        compiler_params=pltpu.CompilerParams(vmem_limit_bytes=8 * MIB),
        cost_estimate=pl.CostEstimate(flops=1, bytes_accessed=1, transcendentals=0),
        name="hidden",
    )(array)


def slot_rows(refs):
    rows = refs[0][...]
    for ref in refs[1:]:
        rows = rows + ref[...]
    return rows


def split(slots, refs):
    groups = []
    for slot in slots:
        groups.append(refs[: len(slot)])
        refs = refs[len(slot) :]
    return groups, refs


def partials(meta, masks, weight, rows, tokens, dtypes, splits, slots=None, turned=None, adds=None, keep=True, after=(), weight_of=1):
    feats = weight.shape[1]
    tile = rows // (4 if keep else 2)
    steps = rows // tile
    total = len(masks) * steps
    depth = 3
    blocks = [in_vmem(block) for slot in slots for block in slot] if slots else [in_vmem(turned)]
    each = tokens // len(slots) if slots else 0
    extra = [a for group in adds or [] for a in group]
    per = len(extra) // len(masks)

    def kernel(meta_ref, w_ref, *refs):
        block_refs, refs = refs[: len(blocks)], refs[len(blocks) :]
        add_refs, refs = refs[: len(extra)], refs[len(extra) :]
        out_refs, refs = refs[: len(masks) * splits], list(refs[len(masks) * splits :])
        turned_ref = refs.pop(0) if slots else block_refs[0]
        kept_ref = refs.pop(0) if keep else w_ref
        k = pl.program_id(0)

        def copy(step):
            block = meta_ref[0] ^ masks[step // steps]
            at = pl.multiple_of(block * rows + step % steps * tile, tile)
            return pltpu.make_async_copy(w_ref.at[pl.ds(at, tile), :], kept_ref.at[pl.ds(step * tile, tile), :], refs[0].at[step])

        @pl.when(k == 0)
        def _():
            if keep:
                for step in range(depth - 1):
                    copy(step).start()
            if slots:
                for n, group in enumerate(split(slots, block_refs)[0]):
                    turned_ref[:, n * each : (n + 1) * each] = slot_rows(group).T

        for step in range(total):
            j, i = step // steps, step % steps

            @pl.when(k == step)
            def _():
                if keep:
                    if step + depth - 1 < total:
                        copy(step + depth - 1).start()
                    copy(step).wait()
                w = kept_ref[step * tile : (step + 1) * tile, :]
                value = jnp.dot(w, turned_ref[...], preferred_element_type=jnp.float32)
                if extra:
                    add_ref, at = add_refs[j * per + i * per // steps], i % (steps // per) * tile
                    value = value + add_ref[at : at + tile, :].astype(jnp.float32)
                at = i % (steps // splits) * tile
                out_refs[j * splits + i * splits // steps][at : at + tile, :] = value.astype(dtypes[j])

    in_place = pl.BlockSpec(memory_space=pltpu.VMEM)
    ins = [in_hbm(weight) if keep else in_vmem(weight), *blocks, *[in_vmem(piece) for piece in extra]]
    outs = [(pltpu.VMEM((rows // splits, tokens), dtype), in_place) for dtype in dtypes for _ in range(splits)]
    scratch = []
    if slots:
        outs.append((pltpu.VMEM((feats, tokens), weight.dtype), in_place))
    if keep:
        outs.append((pltpu.VMEM((total * tile, feats), weight.dtype), in_place))
        scratch = [pltpu.SemaphoreType.DMA((total,))]
    return call(kernel, "partials", meta, (total,), ins, outs, scratch, after=after, weight=weight_of, vmem=8)


def turned_slots(meta, slots, each, feats, after=(), weight=1):
    def kernel(meta_ref, *refs):
        groups, (out_ref,) = split(slots, refs)
        for n, group in enumerate(groups):
            out_ref[:, n * each : (n + 1) * each] = slot_rows(group).T

    outs = [(pltpu.VMEM((feats, len(slots) * each), jnp.bfloat16), pl.BlockSpec(memory_space=pltpu.VMEM))]
    ins = [in_vmem(block) for slot in slots for block in slot]
    return call(kernel, "turned", meta, (1,), ins, outs, after=after, weight=weight, vmem=6)


def all_slots(meta, slots, each, feats, after=()):
    def kernel(meta_ref, *refs):
        groups, (out_ref,) = split(slots, refs)
        for n, group in enumerate(groups):
            out_ref[pl.ds(pl.multiple_of(meta_ref[1 + n] * each, each), each), :] = slot_rows(group)

    outs = [(pltpu.VMEM((len(slots) * each, feats), jnp.bfloat16), pl.BlockSpec(memory_space=pltpu.VMEM))]
    ins = [in_vmem(block) for slot in slots for block in slot]
    return call(kernel, "token_rows", meta, (1,), ins, outs, after=after, vmem=6)


def weight_grad(meta, masks, hiddens, cots, total_rows, after=(), weight=1):
    tokens, feats = cots.shape
    rows = hiddens[0].shape[0]
    steps = 2
    tile = rows // steps
    total = len(masks) * steps

    def kernel(meta_ref, cot_ref, *refs):
        hidden_refs, (out_ref,) = refs[: len(masks)], refs[len(masks) :]
        k = pl.program_id(0)
        for j, ref in enumerate(hidden_refs):

            @pl.when(k // steps == j)
            def _():
                h = ref[pl.ds(pl.multiple_of(lax.rem(k, steps) * tile, tile), tile), :]
                out_ref[...] = jnp.dot(h, cot_ref[...], preferred_element_type=jnp.float32).astype(out_ref.dtype)

    def place(k, m):
        block = m[0] ^ masks[0]
        for j in range(1, len(masks)):
            block = jnp.where(k // steps == j, m[0] ^ masks[j], block)
        return block * steps + k % steps, 0

    return call(
        kernel, "weight_grad", meta, (total,),
        [in_vmem(cots), *[in_vmem(h) for h in hiddens]],
        [(jax.ShapeDtypeStruct((total_rows, feats), cots.dtype), pl.BlockSpec((tile, feats), place))],
        after=after, weight=weight, vmem=20,
    )


def gate_grad(meta, acts, early, weight, turned, back, far, after=()):
    _, rows, tokens = acts.shape
    feats, half = turned.shape
    tile = rows // 4
    per = len(back)

    def kernel(meta_ref, acts_ref, mine_ref, theirs_ref, w_ref, turned_ref, *refs):
        back_refs, far_ref, out_ref = refs[:per], refs[per], refs[per + 1]
        i = pl.program_id(0)
        here = pl.ds(pl.multiple_of(i * tile, tile), tile)
        late = jnp.dot(w_ref[here, :], turned_ref[...], preferred_element_type=jnp.float32)
        late = late + far_ref[here, :].astype(jnp.float32)
        there = pl.ds(pl.multiple_of(i % (4 // per) * tile, tile), tile)
        added = back_refs[0][there, :]
        for p in range(1, per):
            added = jnp.where(i * per // 4 == p, back_refs[p][there, :], added)
        late = late + added.astype(jnp.float32)
        for slot in range(tokens // LANES):
            lanes = slice(slot * LANES % half, slot * LANES % half + LANES)
            if slot * LANES < half:
                grad = mine_ref[here, lanes] + theirs_ref[here, lanes].astype(jnp.float32)
            else:
                grad = late[:, lanes]
            columns = pl.ds(pl.multiple_of(meta_ref[1 + slot] * LANES, LANES), LANES)
            gate = acts_ref[0, here, columns].astype(jnp.float32)
            upper = acts_ref[1, here, columns].astype(jnp.float32)
            sigm = sigmoid(gate)
            out_ref[0, :, columns] = (grad * upper * sigm * (1.0 + gate * (1.0 - sigm))).astype(out_ref.dtype)
            out_ref[1, :, columns] = (grad * (gate * sigm)).astype(out_ref.dtype)

    ins = [in_vmem(a) for a in (acts, *early, weight, turned, *back, far)]
    outs = [(jax.ShapeDtypeStruct(acts.shape, acts.dtype), pl.BlockSpec((2, tile, tokens), lambda i, m: (0, i, 0)))]
    return call(kernel, "gate_grad", meta, (4,), ins, outs, after=after, vmem=12)


def wait_for(meta, after, weight):
    return call(lambda meta_ref: None, "arrived", meta, (1,), [], [], after=after, weight=weight, vmem=1)[0]


ARRIVALS = ((0, 1, 2, 3), (1, 0, 2, 3), (2, 3, 1, 0), (3, 2, 1, 0))


def describe(me, z):
    tables = [np.array([0, *order], np.int32) for order in ARRIVALS]
    meta = jnp.asarray(tables[0])
    for k in range(1, len(tables)):
        meta = jnp.where(z == k, tables[k], meta)
    return meta + me * np.array([1, 0, 0, 0, 0], np.int32)


def two_level(cotangent, down_weight, pre_acts):
    me, z = lax.axis_index("grp"), lax.axis_index("inner")
    total_rows = down_weight.shape[0]
    rows = pre_acts.shape[1]
    each, feats = cotangent.shape
    tokens = 2 * each
    across_core = functools.partial(lax.ppermute, axis_name="grp", perm=[(k, k ^ 1) for k in range(4)])
    across_x = functools.partial(lax.ppermute, axis_name="grp", perm=[(k, k ^ 2) for k in range(4)])
    in_pairs = functools.partial(lax.ppermute, axis_name="inner", perm=[(0, 1), (1, 0), (2, 3), (3, 2)])
    in_middle = functools.partial(lax.ppermute, axis_name="inner", perm=[(1, 2), (2, 1)])
    outwards = functools.partial(lax.ppermute, axis_name="inner", perm=[(1, 0), (2, 3)])
    meta = describe(me, z)
    bf16, f32 = jnp.bfloat16, jnp.float32

    hidden = hidden_rows(pre_acts)
    hidden_far, hidden_core = across_x(hidden), across_core(hidden)

    near, second = in_pairs(cotangent), in_middle(cotangent)
    third, outer = in_middle(near), outwards(second)
    third, outer = lax.optimization_barrier((third, outer))
    outmost = outwards(third)
    slots = [[cotangent], [near], [second, outer], [third, outmost]]

    sums = functools.partial(partials, meta, rows=rows, tokens=tokens)
    turned, _ = turned_slots(meta, slots[:2], each, feats, weight=TURNED)
    *sent, kept_sent, _ = sums((3, 1), down_weight, dtypes=(bf16, bf16), splits=2, turned=turned)
    back = [across_core(p) for p in sent]
    a_sum, kept_sum, done = sums((2,), down_weight, dtypes=(bf16,), splits=1, turned=turned, adds=(back[:2],), after=(hidden_core,))
    a_far = across_x(a_sum)
    a_own, kept_own, done = sums((0,), down_weight, dtypes=(f32,), splits=1, turned=turned, adds=(back[2:],), after=(done,))

    *sent, turned, done = sums(
        (3, 1), kept_sent, dtypes=(bf16, bf16), splits=2, slots=slots[2:], keep=False, after=(done,)
    )
    back = [across_core(p) for p in sent]
    cots, done = all_slots(meta, slots, each, feats, after=(done,))
    hidden_far, done = lax.optimization_barrier((hidden_far, done))
    hidden_both = across_core(hidden_far)
    b_sum, done = sums((2,), kept_sum, dtypes=(bf16,), splits=1, turned=turned, adds=(back[:2],), keep=False, after=(done,))
    b_far = across_x(b_sum)
    done = wait_for(meta, (done, a_far), ARRIVED)
    grad_down, done = weight_grad(
        meta, (0, 1, 2, 3), (hidden, hidden_core, hidden_far, hidden_both), cots, total_rows, after=(done,), weight=200 * 10**9
    )
    grad_pre, _ = gate_grad(meta, pre_acts, (a_own, a_far), kept_own, turned, back[2:], b_far, after=(done,))
    return grad_pre, grad_down


def plain(cotangent, down_weight, pre_acts):
    all_rows = lax.all_gather(cotangent, "inner", axis=0, tiled=True)
    hidden = hidden_of(pre_acts)
    grad = lax.psum_scatter(
        jnp.einsum("fd,td->ft", down_weight, all_rows, preferred_element_type=jnp.float32),
        "grp",
        scatter_dimension=0,
        tiled=True,
    )
    gate = pre_acts[0].astype(jnp.float32)
    upper = pre_acts[1].astype(jnp.float32)
    sigm = jax.nn.sigmoid(gate)
    grad_gate = grad * upper * sigm * (1.0 + gate * (1.0 - sigm))
    grad_pre = jnp.stack([grad_gate, grad * (gate * sigm)]).astype(jnp.bfloat16)
    grad_down = jnp.dot(
        lax.all_gather(hidden, "grp", axis=0, tiled=True), all_rows, preferred_element_type=jnp.float32
    ).astype(jnp.bfloat16)
    return grad_pre, grad_down


def solution(mesh):
    inner, grp = mesh.shape["inner"], mesh.shape["grp"]

    def on_device(cotangent, down_weight, pre_acts):
        if grp == 4 and inner == 4 and cotangent.shape[0] == LANES and pre_acts.shape[1] % 128 == 0:
            return two_level(cotangent, down_weight, pre_acts)
        return plain(cotangent, down_weight, pre_acts)

    return jax.shard_map(
        on_device,
        mesh=mesh,
        in_specs=(
            P(("parts", "inner"), "grp"),
            P("inner", "grp"),
            P(None, ("inner", "grp"), "parts"),
        ),
        out_specs=(P(None, ("inner", "grp"), "parts"), P(("parts", "inner"), "grp")),
        check_vma=False,
    )
```

```python
import functools
import math

import jax
import jax.numpy as jnp
import numpy as np
from jax import lax
from jax.experimental import pallas as pl
from jax.experimental.pallas import tpu as pltpu
from jax.sharding import PartitionSpec as P

LANES = 128
TURNED, ARRIVED = 7000 * 10**6, 9200 * 10**6
MIB = 1024 * 1024


def in_vmem(array):
    return pltpu.with_memory_space_constraint(array, pltpu.VMEM), pl.BlockSpec(memory_space=pltpu.VMEM)


def in_hbm(array):
    return pltpu.with_memory_space_constraint(array, pltpu.HBM), pl.BlockSpec(memory_space=pltpu.HBM)


def anywhere(array):
    return array, pl.BlockSpec(memory_space=pl.ANY)


def sigmoid(x):
    return 0.5 * jnp.tanh(0.5 * x) + 0.5


def hidden_of(acts):
    gate = acts[0].astype(jnp.float32)
    upper = acts[1].astype(jnp.float32)
    return (gate * sigmoid(gate) * upper).astype(jnp.bfloat16)


def tile_of(rows, most):
    return max(t for t in range(16, most + 1, 16) if rows % t == 0)


TOKEN = (pltpu.VMEM((8, LANES), jnp.float32), pl.BlockSpec(memory_space=pltpu.VMEM))


def call(kernel, name, meta, grid, ins, outs, scratch=(), alias=None, after=(), weight=1, vmem=16):
    ins = list(ins) + [anywhere(a) for a in after]
    read = len(ins) - len(after)
    aliases = {}
    if alias is not None:
        aliases = {1 + len(ins): len(outs) - 1}
        ins.append(in_hbm(alias))
    outs = list(outs) + [TOKEN]

    def body(meta_ref, *refs):
        refs = list(refs)
        token = refs.pop(len(ins) + len(outs) - 1)
        token[...] = jnp.zeros_like(token)
        kernel(meta_ref, *refs[:read], *refs[len(ins) :])

    return pl.pallas_call(
        body,
        grid_spec=pltpu.PrefetchScalarGridSpec(
            num_scalar_prefetch=1, grid=grid, in_specs=[s for _, s in ins], out_specs=[s for _, s in outs], scratch_shapes=list(scratch)
        ),
        out_shape=[s for s, _ in outs],
        input_output_aliases=aliases,
        compiler_params=pltpu.CompilerParams(vmem_limit_bytes=vmem * MIB),
        cost_estimate=pl.CostEstimate(flops=weight, bytes_accessed=1, transcendentals=0),
        name=name,
    )(meta, *[a for a, _ in ins])


def hidden_rows(acts):
    _, rows, tokens = acts.shape
    parts = 4
    tile = rows // parts

    def kernel(acts_ref, out_ref, buf, sems):
        def loads(p):
            here = pl.ds(p * tile, tile)
            return [pltpu.make_async_copy(acts_ref.at[n, here, :], buf.at[n, here, :], sems.at[p, n]) for n in range(2)]

        for p in range(parts):
            for load in loads(p):
                load.start()
        for p in range(parts):
            for load in loads(p):
                load.wait()
            for at in range(p * tile, (p + 1) * tile, tile // 2):
                out_ref[pl.ds(at, tile // 2), :] = hidden_of(buf[:, pl.ds(at, tile // 2), :])

    array, spec = in_hbm(acts)
    return pl.pallas_call(
        kernel,
        in_specs=[spec],
        out_specs=pl.BlockSpec(memory_space=pltpu.VMEM),
        out_shape=pltpu.VMEM((rows, tokens), acts.dtype),
        scratch_shapes=[pltpu.VMEM(acts.shape, acts.dtype), pltpu.SemaphoreType.DMA((parts, 2))],
        compiler_params=pltpu.CompilerParams(vmem_limit_bytes=8 * MIB),
        cost_estimate=pl.CostEstimate(flops=1, bytes_accessed=1, transcendentals=0),
        name="hidden",
    )(array)


def slot_rows(refs):
    rows = refs[0][...]
    for ref in refs[1:]:
        rows = rows + ref[...]
    return rows


def split(slots, refs):
    groups = []
    for slot in slots:
        groups.append(refs[: len(slot)])
        refs = refs[len(slot) :]
    return groups, refs


def partials(meta, masks, weight, rows, tokens, dtypes, splits, slots=None, turned=None, adds=None, keep=True, after=(), weight_of=1):
    feats = weight.shape[1]
    tile = rows // (4 if keep else 2)
    steps = rows // tile
    total = len(masks) * steps
    depth = 3
    blocks = [in_vmem(block) for slot in slots for block in slot] if slots else [in_vmem(turned)]
    each = tokens // len(slots) if slots else 0
    extra = [a for group in adds or [] for a in group]

    def overlaps(low, count):
        size = rows // count
        for p in range(count):
            first, last = max(low, p * size), min(low + tile, (p + 1) * size)
            if first < last:
                yield p, slice(first - p * size, last - p * size), slice(first - low, last - low)

    def kernel(meta_ref, w_ref, *refs):
        block_refs, refs = refs[: len(blocks)], refs[len(blocks) :]
        add_refs, refs = refs[: len(extra)], refs[len(extra) :]
        out_refs, refs = refs[: sum(splits)], list(refs[sum(splits) :])
        turned_ref = refs.pop(0) if slots else block_refs[0]
        kept_ref = refs.pop(0) if keep else w_ref
        k = pl.program_id(0)

        def copy(step):
            block = meta_ref[0] ^ masks[step // steps]
            at = pl.multiple_of(block * rows + step % steps * tile, tile)
            return pltpu.make_async_copy(w_ref.at[pl.ds(at, tile), :], kept_ref.at[pl.ds(step * tile, tile), :], refs[0].at[step])

        @pl.when(k == 0)
        def _():
            if keep:
                for step in range(depth - 1):
                    copy(step).start()
            if slots:
                for n, group in enumerate(split(slots, block_refs)[0]):
                    turned_ref[:, n * each : (n + 1) * each] = slot_rows(group).T

        for step in range(total):
            j, i = step // steps, step % steps

            @pl.when(k == step)
            def _():
                if keep:
                    if step + depth - 1 < total:
                        copy(step + depth - 1).start()
                    copy(step).wait()
                w = kept_ref[step * tile : (step + 1) * tile, :]
                value = jnp.dot(w, turned_ref[...], preferred_element_type=jnp.float32)
                if extra:
                    base = sum(len(group) for group in adds[:j])
                    added = [add_refs[base + p][there, :] for p, there, _ in overlaps(i * tile, len(adds[j]))]
                    value = value + jnp.concatenate(added).astype(jnp.float32)
                for p, there, here in overlaps(i * tile, splits[j]):
                    out_refs[sum(splits[:j]) + p][there, :] = value[here, :].astype(dtypes[j])

    in_place = pl.BlockSpec(memory_space=pltpu.VMEM)
    ins = [in_hbm(weight) if keep else in_vmem(weight), *blocks, *[in_vmem(piece) for piece in extra]]
    outs = [(pltpu.VMEM((rows // n, tokens), dtype), in_place) for dtype, n in zip(dtypes, splits, strict=True) for _ in range(n)]
    scratch = []
    if slots:
        outs.append((pltpu.VMEM((feats, tokens), weight.dtype), in_place))
    if keep:
        outs.append((pltpu.VMEM((total * tile, feats), weight.dtype), in_place))
        scratch = [pltpu.SemaphoreType.DMA((total,))]
    return call(kernel, "partials", meta, (total,), ins, outs, scratch, after=after, weight=weight_of, vmem=8)


def turned_slots(meta, slots, each, feats, after=(), weight=1):
    def kernel(meta_ref, *refs):
        groups, (out_ref,) = split(slots, refs)
        for n, group in enumerate(groups):
            out_ref[:, n * each : (n + 1) * each] = slot_rows(group).T

    outs = [(pltpu.VMEM((feats, len(slots) * each), jnp.bfloat16), pl.BlockSpec(memory_space=pltpu.VMEM))]
    ins = [in_vmem(block) for slot in slots for block in slot]
    return call(kernel, "turned", meta, (1,), ins, outs, after=after, weight=weight, vmem=6)


def all_slots(meta, slots, each, feats, after=()):
    def kernel(meta_ref, *refs):
        groups, (out_ref,) = split(slots, refs)
        for n, group in enumerate(groups):
            out_ref[pl.ds(pl.multiple_of(meta_ref[1 + n] * each, each), each), :] = slot_rows(group)

    outs = [(pltpu.VMEM((len(slots) * each, feats), jnp.bfloat16), pl.BlockSpec(memory_space=pltpu.VMEM))]
    ins = [in_vmem(block) for slot in slots for block in slot]
    return call(kernel, "token_rows", meta, (1,), ins, outs, after=after, vmem=6)


def weight_grad(meta, masks, hiddens, cots, total_rows, after=(), weight=1):
    tokens, feats = cots.shape
    rows = hiddens[0].shape[0]
    steps = 2
    tile = rows // steps
    total = len(masks) * steps

    def kernel(meta_ref, cot_ref, *refs):
        hidden_refs, (out_ref,) = refs[: len(masks)], refs[len(masks) :]
        k = pl.program_id(0)
        for j, ref in enumerate(hidden_refs):

            @pl.when(k // steps == j)
            def _():
                h = ref[pl.ds(pl.multiple_of(lax.rem(k, steps) * tile, tile), tile), :]
                out_ref[...] = jnp.dot(h, cot_ref[...], preferred_element_type=jnp.float32).astype(out_ref.dtype)

    def place(k, m):
        block = m[0] ^ masks[0]
        for j in range(1, len(masks)):
            block = jnp.where(k // steps == j, m[0] ^ masks[j], block)
        return block * steps + k % steps, 0

    return call(
        kernel, "weight_grad", meta, (total,),
        [in_vmem(cots), *[in_vmem(h) for h in hiddens]],
        [(jax.ShapeDtypeStruct((total_rows, feats), cots.dtype), pl.BlockSpec((tile, feats), place))],
        after=after, weight=weight, vmem=20,
    )


def gate_grad(meta, acts, early, late, after=()):
    _, rows, tokens = acts.shape
    half = tokens // 2
    tile = rows // 4

    def kernel(meta_ref, acts_ref, *refs):
        pairs, out_ref = (refs[:2], refs[2:4]), refs[4]
        here = pl.ds(pl.multiple_of(pl.program_id(0) * tile, tile), tile)
        for slot in range(tokens // LANES):
            mine_ref, theirs_ref = pairs[slot * LANES // half]
            lanes = slice(slot * LANES % half, slot * LANES % half + LANES)
            columns = pl.ds(pl.multiple_of(meta_ref[1 + slot] * LANES, LANES), LANES)
            grad = mine_ref[here, lanes] + theirs_ref[here, lanes].astype(jnp.float32)
            gate = acts_ref[0, here, columns].astype(jnp.float32)
            upper = acts_ref[1, here, columns].astype(jnp.float32)
            sigm = sigmoid(gate)
            active = gate * sigm
            out_ref[0, :, columns] = (grad * upper * (sigm + active * (1.0 - sigm))).astype(out_ref.dtype)
            out_ref[1, :, columns] = (grad * active).astype(out_ref.dtype)

    ins = [in_vmem(a) for a in (acts, *early, *late)]
    outs = [(jax.ShapeDtypeStruct(acts.shape, acts.dtype), pl.BlockSpec((2, tile, tokens), lambda i, m: (0, i, 0)))]
    return call(kernel, "gate_grad", meta, (4,), ins, outs, after=after, vmem=8)


def wait_for(meta, after, weight):
    return call(lambda meta_ref: None, "arrived", meta, (1,), [], [], after=after, weight=weight, vmem=1)[0]


ARRIVALS = ((0, 1, 2, 3), (1, 0, 2, 3), (2, 3, 1, 0), (3, 2, 1, 0))


def describe(me, z):
    tables = [np.array([0, *order], np.int32) for order in ARRIVALS]
    meta = jnp.asarray(tables[0])
    for k in range(1, len(tables)):
        meta = jnp.where(z == k, tables[k], meta)
    return meta + me * np.array([1, 0, 0, 0, 0], np.int32)


def two_level(cotangent, down_weight, pre_acts):
    me, z = lax.axis_index("grp"), lax.axis_index("inner")
    total_rows = down_weight.shape[0]
    rows = pre_acts.shape[1]
    each, feats = cotangent.shape
    tokens = 2 * each
    across_core = functools.partial(lax.ppermute, axis_name="grp", perm=[(k, k ^ 1) for k in range(4)])
    across_x = functools.partial(lax.ppermute, axis_name="grp", perm=[(k, k ^ 2) for k in range(4)])
    in_pairs = functools.partial(lax.ppermute, axis_name="inner", perm=[(0, 1), (1, 0), (2, 3), (3, 2)])
    in_middle = functools.partial(lax.ppermute, axis_name="inner", perm=[(1, 2), (2, 1)])
    outwards = functools.partial(lax.ppermute, axis_name="inner", perm=[(1, 0), (2, 3)])
    meta = describe(me, z)
    bf16, f32 = jnp.bfloat16, jnp.float32

    hidden = hidden_rows(pre_acts)
    hidden_far, hidden_core = across_x(hidden), across_core(hidden)

    near, second = in_pairs(cotangent), in_middle(cotangent)
    third, outer = in_middle(near), outwards(second)
    third, outer = lax.optimization_barrier((third, outer))
    outmost = outwards(third)
    slots = [[cotangent], [near], [second, outer], [third, outmost]]

    sums = functools.partial(partials, meta, rows=rows, tokens=tokens)
    turned, _ = turned_slots(meta, slots[:2], each, feats, weight=TURNED)
    *sent, kept_sent, _ = sums((3, 1), down_weight, dtypes=(bf16, bf16), splits=(2, 2), turned=turned)
    back = [across_core(p) for p in sent]
    a_sum, kept_sum, done = sums((2,), down_weight, dtypes=(bf16,), splits=(1,), turned=turned, adds=(back[:2],), after=(hidden_core,))
    a_far = across_x(a_sum)
    a_own, kept_own, done = sums((0,), down_weight, dtypes=(f32,), splits=(1,), turned=turned, adds=(back[2:],), after=(done,))

    *sent, turned, done = sums(
        (3, 1), kept_sent, dtypes=(bf16, bf16), splits=(2, 4), slots=slots[2:], keep=False, after=(done,)
    )
    back = [across_core(p) for p in sent]
    cots, done = all_slots(meta, slots, each, feats, after=(done,))
    hidden_far, done = lax.optimization_barrier((hidden_far, done))
    hidden_both = across_core(hidden_far)
    b_sum, done = sums((2,), kept_sum, dtypes=(bf16,), splits=(1,), turned=turned, adds=(back[:2],), keep=False, after=(done,))
    b_far = across_x(b_sum)
    b_own, done = sums((0,), kept_own, dtypes=(f32,), splits=(1,), turned=turned, adds=(back[2:],), keep=False, after=(done,))
    done = wait_for(meta, (done, a_far), ARRIVED)
    grad_down, done = weight_grad(
        meta, (0, 1, 2, 3), (hidden, hidden_core, hidden_far, hidden_both), cots, total_rows, after=(done,), weight=200 * 10**9
    )
    grad_pre, _ = gate_grad(meta, pre_acts, (a_own, a_far), (b_own, b_far), after=(done,))
    return grad_pre, grad_down


def plain(cotangent, down_weight, pre_acts):
    all_rows = lax.all_gather(cotangent, "inner", axis=0, tiled=True)
    hidden = hidden_of(pre_acts)
    grad = lax.psum_scatter(
        jnp.einsum("fd,td->ft", down_weight, all_rows, preferred_element_type=jnp.float32),
        "grp",
        scatter_dimension=0,
        tiled=True,
    )
    gate = pre_acts[0].astype(jnp.float32)
    upper = pre_acts[1].astype(jnp.float32)
    sigm = jax.nn.sigmoid(gate)
    grad_gate = grad * upper * sigm * (1.0 + gate * (1.0 - sigm))
    grad_pre = jnp.stack([grad_gate, grad * (gate * sigm)]).astype(jnp.bfloat16)
    grad_down = jnp.dot(
        lax.all_gather(hidden, "grp", axis=0, tiled=True), all_rows, preferred_element_type=jnp.float32
    ).astype(jnp.bfloat16)
    return grad_pre, grad_down


def solution(mesh):
    inner, grp = mesh.shape["inner"], mesh.shape["grp"]

    def on_device(cotangent, down_weight, pre_acts):
        if grp == 4 and inner == 4 and cotangent.shape[0] == LANES and pre_acts.shape[1] % 128 == 0:
            return two_level(cotangent, down_weight, pre_acts)
        return plain(cotangent, down_weight, pre_acts)

    return jax.shard_map(
        on_device,
        mesh=mesh,
        in_specs=(
            P(("parts", "inner"), "grp"),
            P("inner", "grp"),
            P(None, ("inner", "grp"), "parts"),
        ),
        out_specs=(P(None, ("inner", "grp"), "parts"), P(("parts", "inner"), "grp")),
        check_vma=False,
    )
```

```python
import functools
import math

import jax
import jax.numpy as jnp
import numpy as np
from jax import lax
from jax.experimental import pallas as pl
from jax.experimental.pallas import tpu as pltpu
from jax.sharding import PartitionSpec as P

LANES = 128
TURNED, ARRIVED = 7000 * 10**6, 14200 * 10**6
MIB = 1024 * 1024


def in_vmem(array):
    return pltpu.with_memory_space_constraint(array, pltpu.VMEM), pl.BlockSpec(memory_space=pltpu.VMEM)


def in_hbm(array):
    return pltpu.with_memory_space_constraint(array, pltpu.HBM), pl.BlockSpec(memory_space=pltpu.HBM)


def anywhere(array):
    return array, pl.BlockSpec(memory_space=pl.ANY)


def sigmoid(x):
    return 0.5 * jnp.tanh(0.5 * x) + 0.5


def hidden_of(acts):
    gate = acts[0].astype(jnp.float32)
    upper = acts[1].astype(jnp.float32)
    return (gate * sigmoid(gate) * upper).astype(jnp.bfloat16)


def tile_of(rows, most):
    return max(t for t in range(16, most + 1, 16) if rows % t == 0)


TOKEN = (pltpu.VMEM((8, LANES), jnp.float32), pl.BlockSpec(memory_space=pltpu.VMEM))


def call(kernel, name, meta, grid, ins, outs, scratch=(), alias=None, after=(), weight=1, vmem=16):
    ins = list(ins) + [anywhere(a) for a in after]
    read = len(ins) - len(after)
    aliases = {}
    if alias is not None:
        aliases = {1 + len(ins): len(outs) - 1}
        ins.append(in_hbm(alias))
    outs = list(outs) + [TOKEN]

    def body(meta_ref, *refs):
        refs = list(refs)
        token = refs.pop(len(ins) + len(outs) - 1)
        token[...] = jnp.zeros_like(token)
        kernel(meta_ref, *refs[:read], *refs[len(ins) :])

    return pl.pallas_call(
        body,
        grid_spec=pltpu.PrefetchScalarGridSpec(
            num_scalar_prefetch=1, grid=grid, in_specs=[s for _, s in ins], out_specs=[s for _, s in outs], scratch_shapes=list(scratch)
        ),
        out_shape=[s for s, _ in outs],
        input_output_aliases=aliases,
        compiler_params=pltpu.CompilerParams(vmem_limit_bytes=vmem * MIB),
        cost_estimate=pl.CostEstimate(flops=weight, bytes_accessed=1, transcendentals=0),
        name=name,
    )(meta, *[a for a, _ in ins])


def hidden_rows(acts):
    _, rows, tokens = acts.shape
    parts = 4
    tile = rows // parts

    def kernel(acts_ref, out_ref, buf, sems):
        def loads(p):
            here = pl.ds(p * tile, tile)
            return [pltpu.make_async_copy(acts_ref.at[n, here, :], buf.at[n, here, :], sems.at[p, n]) for n in range(2)]

        for p in range(parts):
            for load in loads(p):
                load.start()
        for p in range(parts):
            for load in loads(p):
                load.wait()
            for at in range(p * tile, (p + 1) * tile, tile // 2):
                out_ref[pl.ds(at, tile // 2), :] = hidden_of(buf[:, pl.ds(at, tile // 2), :])

    array, spec = in_hbm(acts)
    return pl.pallas_call(
        kernel,
        in_specs=[spec],
        out_specs=pl.BlockSpec(memory_space=pltpu.VMEM),
        out_shape=pltpu.VMEM((rows, tokens), acts.dtype),
        scratch_shapes=[pltpu.VMEM(acts.shape, acts.dtype), pltpu.SemaphoreType.DMA((parts, 2))],
        compiler_params=pltpu.CompilerParams(vmem_limit_bytes=8 * MIB),
        cost_estimate=pl.CostEstimate(flops=1, bytes_accessed=1, transcendentals=0),
        name="hidden",
    )(array)


def slot_rows(refs):
    rows = refs[0][...]
    for ref in refs[1:]:
        rows = rows + ref[...]
    return rows


def split(slots, refs):
    groups = []
    for slot in slots:
        groups.append(refs[: len(slot)])
        refs = refs[len(slot) :]
    return groups, refs


def partials(meta, masks, weight, rows, tokens, dtypes, splits, slots=None, turned=None, adds=None, keep=True, after=(), weight_of=1):
    feats = weight.shape[1]
    tile = rows // (4 if keep else 2)
    steps = rows // tile
    total = len(masks) * steps
    depth = 3
    blocks = [in_vmem(block) for slot in slots for block in slot] if slots else [in_vmem(turned)]
    each = tokens // len(slots) if slots else 0
    extra = [a for group in adds or [] for a in group]

    def overlaps(low, count):
        size = rows // count
        for p in range(count):
            first, last = max(low, p * size), min(low + tile, (p + 1) * size)
            if first < last:
                yield p, slice(first - p * size, last - p * size), slice(first - low, last - low)

    def kernel(meta_ref, w_ref, *refs):
        block_refs, refs = refs[: len(blocks)], refs[len(blocks) :]
        add_refs, refs = refs[: len(extra)], refs[len(extra) :]
        out_refs, refs = refs[: sum(splits)], list(refs[sum(splits) :])
        turned_ref = refs.pop(0) if slots else block_refs[0]
        kept_ref = refs.pop(0) if keep else w_ref
        k = pl.program_id(0)

        def copy(step):
            block = meta_ref[0] ^ masks[step // steps]
            at = pl.multiple_of(block * rows + step % steps * tile, tile)
            return pltpu.make_async_copy(w_ref.at[pl.ds(at, tile), :], kept_ref.at[pl.ds(step * tile, tile), :], refs[0].at[step])

        @pl.when(k == 0)
        def _():
            if keep:
                for step in range(depth - 1):
                    copy(step).start()
            if slots:
                for n, group in enumerate(split(slots, block_refs)[0]):
                    turned_ref[:, n * each : (n + 1) * each] = slot_rows(group).T

        for step in range(total):
            j, i = step // steps, step % steps

            @pl.when(k == step)
            def _():
                if keep:
                    if step + depth - 1 < total:
                        copy(step + depth - 1).start()
                    copy(step).wait()
                w = kept_ref[step * tile : (step + 1) * tile, :]
                value = jnp.dot(w, turned_ref[...], preferred_element_type=jnp.float32)
                if extra:
                    base = sum(len(group) for group in adds[:j])
                    added = [add_refs[base + p][there, :] for p, there, _ in overlaps(i * tile, len(adds[j]))]
                    value = value + jnp.concatenate(added).astype(jnp.float32)
                for p, there, here in overlaps(i * tile, splits[j]):
                    out_refs[sum(splits[:j]) + p][there, :] = value[here, :].astype(dtypes[j])

    in_place = pl.BlockSpec(memory_space=pltpu.VMEM)
    ins = [in_hbm(weight) if keep else in_vmem(weight), *blocks, *[in_vmem(piece) for piece in extra]]
    outs = [(pltpu.VMEM((rows // n, tokens), dtype), in_place) for dtype, n in zip(dtypes, splits, strict=True) for _ in range(n)]
    scratch = []
    if slots:
        outs.append((pltpu.VMEM((feats, tokens), weight.dtype), in_place))
    if keep:
        outs.append((pltpu.VMEM((total * tile, feats), weight.dtype), in_place))
        scratch = [pltpu.SemaphoreType.DMA((total,))]
    return call(kernel, "partials", meta, (total,), ins, outs, scratch, after=after, weight=weight_of, vmem=8)


def turned_slots(meta, slots, each, feats, after=(), weight=1):
    def kernel(meta_ref, *refs):
        groups, (out_ref,) = split(slots, refs)
        for n, group in enumerate(groups):
            out_ref[:, n * each : (n + 1) * each] = slot_rows(group).T

    outs = [(pltpu.VMEM((feats, len(slots) * each), jnp.bfloat16), pl.BlockSpec(memory_space=pltpu.VMEM))]
    ins = [in_vmem(block) for slot in slots for block in slot]
    return call(kernel, "turned", meta, (1,), ins, outs, after=after, weight=weight, vmem=6)


def all_slots(meta, slots, each, feats, after=()):
    def kernel(meta_ref, *refs):
        groups, (out_ref,) = split(slots, refs)
        for n, group in enumerate(groups):
            out_ref[pl.ds(pl.multiple_of(meta_ref[1 + n] * each, each), each), :] = slot_rows(group)

    outs = [(pltpu.VMEM((len(slots) * each, feats), jnp.bfloat16), pl.BlockSpec(memory_space=pltpu.VMEM))]
    ins = [in_vmem(block) for slot in slots for block in slot]
    return call(kernel, "token_rows", meta, (1,), ins, outs, after=after, vmem=6)


def weight_grad(meta, masks, hiddens, cots, total_rows, after=(), weight=1):
    tokens, feats = cots.shape
    rows = hiddens[0].shape[0]
    steps = 2
    tile = rows // steps
    total = len(masks) * steps

    def kernel(meta_ref, cot_ref, *refs):
        hidden_refs, (out_ref,) = refs[: len(masks)], refs[len(masks) :]
        k = pl.program_id(0)
        for j, ref in enumerate(hidden_refs):

            @pl.when(k // steps == j)
            def _():
                h = ref[pl.ds(pl.multiple_of(lax.rem(k, steps) * tile, tile), tile), :]
                out_ref[...] = jnp.dot(h, cot_ref[...], preferred_element_type=jnp.float32).astype(out_ref.dtype)

    def place(k, m):
        block = m[0] ^ masks[0]
        for j in range(1, len(masks)):
            block = jnp.where(k // steps == j, m[0] ^ masks[j], block)
        return block * steps + k % steps, 0

    return call(
        kernel, "weight_grad", meta, (total,),
        [in_vmem(cots), *[in_vmem(h) for h in hiddens]],
        [(jax.ShapeDtypeStruct((total_rows, feats), cots.dtype), pl.BlockSpec((tile, feats), place))],
        after=after, weight=weight, vmem=20,
    )


def gate_grad(meta, acts, early, late, after=()):
    _, rows, tokens = acts.shape
    half = tokens // 2
    tile = rows // 2

    def kernel(meta_ref, acts_ref, *refs):
        pairs, out_ref = (refs[:2], refs[2:4]), refs[4]
        here = pl.ds(pl.multiple_of(pl.program_id(0) * tile, tile), tile)
        for slot in range(tokens // LANES):
            mine_ref, theirs_ref = pairs[slot * LANES // half]
            lanes = slice(slot * LANES % half, slot * LANES % half + LANES)
            columns = pl.ds(pl.multiple_of(meta_ref[1 + slot] * LANES, LANES), LANES)
            grad = mine_ref[here, lanes] + theirs_ref[here, lanes].astype(jnp.float32)
            gate = acts_ref[0, here, columns].astype(jnp.float32)
            upper = acts_ref[1, here, columns].astype(jnp.float32)
            sigm = sigmoid(gate)
            active = gate * sigm
            out_ref[0, :, columns] = (grad * upper * (sigm + active * (1.0 - sigm))).astype(out_ref.dtype)
            out_ref[1, :, columns] = (grad * active).astype(out_ref.dtype)

    ins = [in_vmem(a) for a in (acts, *early, *late)]
    outs = [(jax.ShapeDtypeStruct(acts.shape, acts.dtype), pl.BlockSpec((2, tile, tokens), lambda i, m: (0, i, 0)))]
    return call(kernel, "gate_grad", meta, (2,), ins, outs, after=after, vmem=8)


def wait_for(meta, after, weight):
    return call(lambda meta_ref: None, "arrived", meta, (1,), [], [], after=after, weight=weight, vmem=1)[0]


ARRIVALS = ((0, 1, 2, 3), (1, 0, 2, 3), (2, 3, 1, 0), (3, 2, 1, 0))


def describe(me, z):
    tables = [np.array([0, *order], np.int32) for order in ARRIVALS]
    meta = jnp.asarray(tables[0])
    for k in range(1, len(tables)):
        meta = jnp.where(z == k, tables[k], meta)
    return meta + me * np.array([1, 0, 0, 0, 0], np.int32)


def two_level(cotangent, down_weight, pre_acts):
    me, z = lax.axis_index("grp"), lax.axis_index("inner")
    total_rows = down_weight.shape[0]
    rows = pre_acts.shape[1]
    each, feats = cotangent.shape
    tokens = 2 * each
    across_core = functools.partial(lax.ppermute, axis_name="grp", perm=[(k, k ^ 1) for k in range(4)])
    across_x = functools.partial(lax.ppermute, axis_name="grp", perm=[(k, k ^ 2) for k in range(4)])
    in_pairs = functools.partial(lax.ppermute, axis_name="inner", perm=[(0, 1), (1, 0), (2, 3), (3, 2)])
    in_middle = functools.partial(lax.ppermute, axis_name="inner", perm=[(1, 2), (2, 1)])
    outwards = functools.partial(lax.ppermute, axis_name="inner", perm=[(1, 0), (2, 3)])
    meta = describe(me, z)
    bf16, f32 = jnp.bfloat16, jnp.float32

    hidden = hidden_rows(pre_acts)
    hidden_far, hidden_core = across_x(hidden), across_core(hidden)

    near, second = in_pairs(cotangent), in_middle(cotangent)
    third, outer = in_middle(near), outwards(second)
    third, outer = lax.optimization_barrier((third, outer))
    outmost = outwards(third)
    slots = [[cotangent], [near], [second, outer], [third, outmost]]

    sums = functools.partial(partials, meta, rows=rows, tokens=tokens)
    turned, _ = turned_slots(meta, slots[:2], each, feats, weight=TURNED)
    *sent, kept_sent, _ = sums((3, 1), down_weight, dtypes=(bf16, bf16), splits=(2, 2), turned=turned)
    back = [across_core(p) for p in sent]
    a_sum, kept_sum, done = sums((2,), down_weight, dtypes=(bf16,), splits=(1,), turned=turned, adds=(back[:2],), after=(hidden_core,))
    a_far = across_x(a_sum)
    a_own, kept_own, done = sums((0,), down_weight, dtypes=(f32,), splits=(1,), turned=turned, adds=(back[2:],), after=(done,))

    *sent, turned, done = sums(
        (3, 1), kept_sent, dtypes=(bf16, bf16), splits=(2, 4), slots=slots[2:], keep=False, after=(done,)
    )
    back = [across_core(p) for p in sent]
    cots, done = all_slots(meta, slots, each, feats, after=(done,))
    hidden_far, back[0], back[1] = lax.optimization_barrier((hidden_far, back[0], back[1]))
    hidden_both = across_core(hidden_far)
    b_sum, done = sums((2,), kept_sum, dtypes=(bf16,), splits=(1,), turned=turned, adds=(back[:2],), keep=False, after=(done,))
    b_far = across_x(b_sum)
    b_own, done = sums((0,), kept_own, dtypes=(f32,), splits=(1,), turned=turned, adds=(back[2:],), keep=False, after=(done,))
    done = wait_for(meta, (done, a_far), ARRIVED)
    grad_down, done = weight_grad(
        meta, (0, 1, 2, 3), (hidden, hidden_core, hidden_far, hidden_both), cots, total_rows, after=(done,), weight=200 * 10**9
    )
    grad_pre, _ = gate_grad(meta, pre_acts, (a_own, a_far), (b_own, b_far), after=(done,))
    return grad_pre, grad_down


def plain(cotangent, down_weight, pre_acts):
    all_rows = lax.all_gather(cotangent, "inner", axis=0, tiled=True)
    hidden = hidden_of(pre_acts)
    grad = lax.psum_scatter(
        jnp.einsum("fd,td->ft", down_weight, all_rows, preferred_element_type=jnp.float32),
        "grp",
        scatter_dimension=0,
        tiled=True,
    )
    gate = pre_acts[0].astype(jnp.float32)
    upper = pre_acts[1].astype(jnp.float32)
    sigm = jax.nn.sigmoid(gate)
    grad_gate = grad * upper * sigm * (1.0 + gate * (1.0 - sigm))
    grad_pre = jnp.stack([grad_gate, grad * (gate * sigm)]).astype(jnp.bfloat16)
    grad_down = jnp.dot(
        lax.all_gather(hidden, "grp", axis=0, tiled=True), all_rows, preferred_element_type=jnp.float32
    ).astype(jnp.bfloat16)
    return grad_pre, grad_down


def solution(mesh):
    inner, grp = mesh.shape["inner"], mesh.shape["grp"]

    def on_device(cotangent, down_weight, pre_acts):
        if grp == 4 and inner == 4 and cotangent.shape[0] == LANES and pre_acts.shape[1] % 128 == 0:
            return two_level(cotangent, down_weight, pre_acts)
        return plain(cotangent, down_weight, pre_acts)

    return jax.shard_map(
        on_device,
        mesh=mesh,
        in_specs=(
            P(("parts", "inner"), "grp"),
            P("inner", "grp"),
            P(None, ("inner", "grp"), "parts"),
        ),
        out_specs=(P(None, ("inner", "grp"), "parts"), P(("parts", "inner"), "grp")),
        check_vma=False,
    )
```

```python
import functools
import math

import jax
import jax.numpy as jnp
import numpy as np
from jax import lax
from jax.experimental import pallas as pl
from jax.experimental.pallas import tpu as pltpu
from jax.sharding import PartitionSpec as P

LANES = 128
TURNED, ARRIVED = 7000 * 10**6, 14200 * 10**6
MIB = 1024 * 1024


def in_vmem(array):
    return pltpu.with_memory_space_constraint(array, pltpu.VMEM), pl.BlockSpec(memory_space=pltpu.VMEM)


def in_hbm(array):
    return pltpu.with_memory_space_constraint(array, pltpu.HBM), pl.BlockSpec(memory_space=pltpu.HBM)


def anywhere(array):
    return array, pl.BlockSpec(memory_space=pl.ANY)


def sigmoid(x):
    return 0.5 * jnp.tanh(0.5 * x) + 0.5


def hidden_of(acts):
    gate = acts[0].astype(jnp.float32)
    upper = acts[1].astype(jnp.float32)
    return (gate * sigmoid(gate) * upper).astype(jnp.bfloat16)


def tile_of(rows, most):
    return max(t for t in range(16, most + 1, 16) if rows % t == 0)


TOKEN = (pltpu.VMEM((8, LANES), jnp.float32), pl.BlockSpec(memory_space=pltpu.VMEM))


def call(kernel, name, meta, grid, ins, outs, scratch=(), alias=None, after=(), weight=1, vmem=16):
    heads = [] if meta is None else [meta]
    ins = list(ins) + [anywhere(a) for a in after]
    read = len(ins) - len(after)
    aliases = {}
    if alias is not None:
        aliases = {len(heads) + len(ins): len(outs) - 1}
        ins.append(in_hbm(alias))
    outs = list(outs) + [TOKEN]

    def body(*refs):
        refs = list(refs)
        meta_ref = refs.pop(0) if heads else None
        token = refs.pop(len(ins) + len(outs) - 1)
        token[...] = jnp.zeros_like(token)
        kernel(meta_ref, *refs[:read], *refs[len(ins) :])

    return pl.pallas_call(
        body,
        grid_spec=pltpu.PrefetchScalarGridSpec(
            num_scalar_prefetch=len(heads), grid=grid, in_specs=[s for _, s in ins], out_specs=[s for _, s in outs], scratch_shapes=list(scratch)
        ),
        out_shape=[s for s, _ in outs],
        input_output_aliases=aliases,
        compiler_params=pltpu.CompilerParams(vmem_limit_bytes=vmem * MIB),
        cost_estimate=pl.CostEstimate(flops=weight, bytes_accessed=1, transcendentals=0),
        name=name,
    )(*heads, *[a for a, _ in ins])


def hidden_rows(acts):
    _, rows, tokens = acts.shape
    parts = 4
    tile = rows // parts

    def kernel(acts_ref, out_ref, buf, sems):
        def loads(p):
            here = pl.ds(p * tile, tile)
            return [pltpu.make_async_copy(acts_ref.at[n, here, :], buf.at[n, here, :], sems.at[p, n]) for n in range(2)]

        for p in range(parts):
            for load in loads(p):
                load.start()
        for p in range(parts):
            for load in loads(p):
                load.wait()
            for at in range(p * tile, (p + 1) * tile, tile // 2):
                out_ref[pl.ds(at, tile // 2), :] = hidden_of(buf[:, pl.ds(at, tile // 2), :])

    array, spec = in_hbm(acts)
    return pl.pallas_call(
        kernel,
        in_specs=[spec],
        out_specs=pl.BlockSpec(memory_space=pltpu.VMEM),
        out_shape=pltpu.VMEM((rows, tokens), acts.dtype),
        scratch_shapes=[pltpu.VMEM(acts.shape, acts.dtype), pltpu.SemaphoreType.DMA((parts, 2))],
        compiler_params=pltpu.CompilerParams(vmem_limit_bytes=8 * MIB),
        cost_estimate=pl.CostEstimate(flops=1, bytes_accessed=1, transcendentals=0),
        name="hidden",
    )(array)


def slot_rows(refs):
    rows = refs[0][...]
    for ref in refs[1:]:
        rows = rows + ref[...]
    return rows


def split(slots, refs):
    groups = []
    for slot in slots:
        groups.append(refs[: len(slot)])
        refs = refs[len(slot) :]
    return groups, refs


def partials(meta, masks, weight, rows, tokens, dtypes, splits, slots=None, turned=None, adds=None, keep=True, after=(), weight_of=1):
    feats = weight.shape[1]
    tile = rows // (4 if keep else 2)
    steps = rows // tile
    total = len(masks) * steps
    depth = 3
    blocks = [in_vmem(block) for slot in slots for block in slot] if slots else [in_vmem(turned)]
    each = tokens // len(slots) if slots else 0
    extra = [a for group in adds or [] for a in group]

    def overlaps(low, count):
        size = rows // count
        for p in range(count):
            first, last = max(low, p * size), min(low + tile, (p + 1) * size)
            if first < last:
                yield p, slice(first - p * size, last - p * size), slice(first - low, last - low)

    def kernel(meta_ref, w_ref, *refs):
        block_refs, refs = refs[: len(blocks)], refs[len(blocks) :]
        add_refs, refs = refs[: len(extra)], refs[len(extra) :]
        out_refs, refs = refs[: sum(splits)], list(refs[sum(splits) :])
        turned_ref = refs.pop(0) if slots else block_refs[0]
        kept_ref = refs.pop(0) if keep else w_ref
        k = pl.program_id(0)

        def copy(step):
            block = meta_ref[0] ^ masks[step // steps]
            at = pl.multiple_of(block * rows + step % steps * tile, tile)
            return pltpu.make_async_copy(w_ref.at[pl.ds(at, tile), :], kept_ref.at[pl.ds(step * tile, tile), :], refs[0].at[step])

        @pl.when(k == 0)
        def _():
            if keep:
                for step in range(depth - 1):
                    copy(step).start()
            if slots:
                for n, group in enumerate(split(slots, block_refs)[0]):
                    turned_ref[:, n * each : (n + 1) * each] = slot_rows(group).T

        for step in range(total):
            j, i = step // steps, step % steps

            @pl.when(k == step)
            def _():
                if keep:
                    if step + depth - 1 < total:
                        copy(step + depth - 1).start()
                    copy(step).wait()
                w = kept_ref[step * tile : (step + 1) * tile, :]
                value = jnp.dot(w, turned_ref[...], preferred_element_type=jnp.float32)
                if extra:
                    base = sum(len(group) for group in adds[:j])
                    added = [add_refs[base + p][there, :] for p, there, _ in overlaps(i * tile, len(adds[j]))]
                    value = value + jnp.concatenate(added).astype(jnp.float32)
                for p, there, here in overlaps(i * tile, splits[j]):
                    out_refs[sum(splits[:j]) + p][there, :] = value[here, :].astype(dtypes[j])

    in_place = pl.BlockSpec(memory_space=pltpu.VMEM)
    ins = [in_hbm(weight) if keep else in_vmem(weight), *blocks, *[in_vmem(piece) for piece in extra]]
    outs = [(pltpu.VMEM((rows // n, tokens), dtype), in_place) for dtype, n in zip(dtypes, splits, strict=True) for _ in range(n)]
    scratch = []
    if slots:
        outs.append((pltpu.VMEM((feats, tokens), weight.dtype), in_place))
    if keep:
        outs.append((pltpu.VMEM((total * tile, feats), weight.dtype), in_place))
        scratch = [pltpu.SemaphoreType.DMA((total,))]
    return call(kernel, "partials", meta if keep else None, (total,), ins, outs, scratch, after=after, weight=weight_of, vmem=8)


def turned_slots(meta, slots, each, feats, after=(), weight=1):
    def kernel(meta_ref, *refs):
        groups, (out_ref,) = split(slots, refs)
        for n, group in enumerate(groups):
            out_ref[:, n * each : (n + 1) * each] = slot_rows(group).T

    outs = [(pltpu.VMEM((feats, len(slots) * each), jnp.bfloat16), pl.BlockSpec(memory_space=pltpu.VMEM))]
    ins = [in_vmem(block) for slot in slots for block in slot]
    return call(kernel, "turned", meta, (1,), ins, outs, after=after, weight=weight, vmem=6)


def all_slots(meta, slots, each, feats, after=()):
    def kernel(meta_ref, *refs):
        groups, (out_ref,) = split(slots, refs)
        for n, group in enumerate(groups):
            out_ref[pl.ds(pl.multiple_of(meta_ref[1 + n] * each, each), each), :] = slot_rows(group)

    outs = [(pltpu.VMEM((len(slots) * each, feats), jnp.bfloat16), pl.BlockSpec(memory_space=pltpu.VMEM))]
    ins = [in_vmem(block) for slot in slots for block in slot]
    return call(kernel, "token_rows", meta, (1,), ins, outs, after=after, vmem=6)


def weight_grad(meta, masks, hiddens, cots, total_rows, after=(), weight=1):
    tokens, feats = cots.shape
    rows = hiddens[0].shape[0]
    steps = 2
    tile = rows // steps
    total = len(masks) * steps

    def kernel(meta_ref, cot_ref, *refs):
        hidden_refs, (out_ref,) = refs[: len(masks)], refs[len(masks) :]
        k = pl.program_id(0)
        for j, ref in enumerate(hidden_refs):

            @pl.when(k // steps == j)
            def _():
                h = ref[pl.ds(pl.multiple_of(lax.rem(k, steps) * tile, tile), tile), :]
                out_ref[...] = jnp.dot(h, cot_ref[...], preferred_element_type=jnp.float32).astype(out_ref.dtype)

    def place(k, m):
        block = m[0] ^ masks[0]
        for j in range(1, len(masks)):
            block = jnp.where(k // steps == j, m[0] ^ masks[j], block)
        return block * steps + k % steps, 0

    return call(
        kernel, "weight_grad", meta, (total,),
        [in_vmem(cots), *[in_vmem(h) for h in hiddens]],
        [(jax.ShapeDtypeStruct((total_rows, feats), cots.dtype), pl.BlockSpec((tile, feats), place))],
        after=after, weight=weight, vmem=20,
    )


def gate_grad(meta, acts, early, late, after=()):
    _, rows, tokens = acts.shape
    half = tokens // 2
    tile = rows // 2

    def kernel(meta_ref, acts_ref, *refs):
        pairs, out_ref = (refs[:2], refs[2:4]), refs[4]
        here = pl.ds(pl.multiple_of(pl.program_id(0) * tile, tile), tile)
        for slot in range(tokens // LANES):
            mine_ref, theirs_ref = pairs[slot * LANES // half]
            lanes = slice(slot * LANES % half, slot * LANES % half + LANES)
            columns = pl.ds(pl.multiple_of(meta_ref[1 + slot] * LANES, LANES), LANES)
            grad = mine_ref[here, lanes] + theirs_ref[here, lanes].astype(jnp.float32)
            gate = acts_ref[0, here, columns].astype(jnp.float32)
            upper = acts_ref[1, here, columns].astype(jnp.float32)
            sigm = sigmoid(gate)
            active = gate * sigm
            out_ref[0, :, columns] = (grad * upper * (sigm + active * (1.0 - sigm))).astype(out_ref.dtype)
            out_ref[1, :, columns] = (grad * active).astype(out_ref.dtype)

    ins = [in_vmem(a) for a in (acts, *early, *late)]
    outs = [(jax.ShapeDtypeStruct(acts.shape, acts.dtype), pl.BlockSpec((2, tile, tokens), lambda i, m: (0, i, 0)))]
    return call(kernel, "gate_grad", meta, (2,), ins, outs, after=after, vmem=8)


def wait_for(meta, after, weight):
    return call(lambda meta_ref: None, "arrived", None, (1,), [], [], after=after, weight=weight, vmem=1)[0]


ARRIVALS = ((0, 1, 2, 3), (1, 0, 2, 3), (2, 3, 1, 0), (3, 2, 1, 0))


def describe(me, z):
    tables = [np.array([0, *order], np.int32) for order in ARRIVALS]
    meta = jnp.asarray(tables[0])
    for k in range(1, len(tables)):
        meta = jnp.where(z == k, tables[k], meta)
    return meta + me * np.array([1, 0, 0, 0, 0], np.int32)


def two_level(cotangent, down_weight, pre_acts):
    me, z = lax.axis_index("grp"), lax.axis_index("inner")
    total_rows = down_weight.shape[0]
    rows = pre_acts.shape[1]
    each, feats = cotangent.shape
    tokens = 2 * each
    across_core = functools.partial(lax.ppermute, axis_name="grp", perm=[(k, k ^ 1) for k in range(4)])
    across_x = functools.partial(lax.ppermute, axis_name="grp", perm=[(k, k ^ 2) for k in range(4)])
    in_pairs = functools.partial(lax.ppermute, axis_name="inner", perm=[(0, 1), (1, 0), (2, 3), (3, 2)])
    in_middle = functools.partial(lax.ppermute, axis_name="inner", perm=[(1, 2), (2, 1)])
    outwards = functools.partial(lax.ppermute, axis_name="inner", perm=[(1, 0), (2, 3)])
    meta = describe(me, z)
    bf16, f32 = jnp.bfloat16, jnp.float32

    hidden = hidden_rows(pre_acts)
    hidden_far, hidden_core = across_x(hidden), across_core(hidden)

    near, second = in_pairs(cotangent), in_middle(cotangent)
    third, outer = in_middle(near), outwards(second)
    third, outer = lax.optimization_barrier((third, outer))
    outmost = outwards(third)
    slots = [[cotangent], [near], [second, outer], [third, outmost]]

    sums = functools.partial(partials, meta, rows=rows, tokens=tokens)
    turned, _ = turned_slots(meta, slots[:2], each, feats, weight=TURNED)
    *sent, kept_sent, _ = sums((3, 1), down_weight, dtypes=(bf16, bf16), splits=(2, 2), turned=turned)
    back = [across_core(p) for p in sent]
    a_sum, kept_sum, done = sums((2,), down_weight, dtypes=(bf16,), splits=(1,), turned=turned, adds=(back[:2],), after=(hidden_core,))
    a_far = across_x(a_sum)
    a_own, kept_own, done = sums((0,), down_weight, dtypes=(f32,), splits=(1,), turned=turned, adds=(back[2:],), after=(done,))

    *sent, turned, done = sums(
        (3, 1), kept_sent, dtypes=(bf16, bf16), splits=(2, 4), slots=slots[2:], keep=False, after=(done,)
    )
    back = [across_core(p) for p in sent]
    cots, done = all_slots(meta, slots, each, feats, after=(done,))
    hidden_far, back[0], back[1] = lax.optimization_barrier((hidden_far, back[0], back[1]))
    hidden_both = across_core(hidden_far)
    b_sum, done = sums((2,), kept_sum, dtypes=(bf16,), splits=(1,), turned=turned, adds=(back[:2],), keep=False, after=(done,))
    b_far = across_x(b_sum)
    b_own, done = sums((0,), kept_own, dtypes=(f32,), splits=(1,), turned=turned, adds=(back[2:],), keep=False, after=(done,))
    done = wait_for(meta, (done, a_far), ARRIVED)
    grad_down, done = weight_grad(
        meta, (0, 1, 2, 3), (hidden, hidden_core, hidden_far, hidden_both), cots, total_rows, after=(done,), weight=200 * 10**9
    )
    grad_pre, _ = gate_grad(meta, pre_acts, (a_own, a_far), (b_own, b_far), after=(done,))
    return grad_pre, grad_down


def plain(cotangent, down_weight, pre_acts):
    all_rows = lax.all_gather(cotangent, "inner", axis=0, tiled=True)
    hidden = hidden_of(pre_acts)
    grad = lax.psum_scatter(
        jnp.einsum("fd,td->ft", down_weight, all_rows, preferred_element_type=jnp.float32),
        "grp",
        scatter_dimension=0,
        tiled=True,
    )
    gate = pre_acts[0].astype(jnp.float32)
    upper = pre_acts[1].astype(jnp.float32)
    sigm = jax.nn.sigmoid(gate)
    grad_gate = grad * upper * sigm * (1.0 + gate * (1.0 - sigm))
    grad_pre = jnp.stack([grad_gate, grad * (gate * sigm)]).astype(jnp.bfloat16)
    grad_down = jnp.dot(
        lax.all_gather(hidden, "grp", axis=0, tiled=True), all_rows, preferred_element_type=jnp.float32
    ).astype(jnp.bfloat16)
    return grad_pre, grad_down


def solution(mesh):
    inner, grp = mesh.shape["inner"], mesh.shape["grp"]

    def on_device(cotangent, down_weight, pre_acts):
        if grp == 4 and inner == 4 and cotangent.shape[0] == LANES and pre_acts.shape[1] % 128 == 0:
            return two_level(cotangent, down_weight, pre_acts)
        return plain(cotangent, down_weight, pre_acts)

    return jax.shard_map(
        on_device,
        mesh=mesh,
        in_specs=(
            P(("parts", "inner"), "grp"),
            P("inner", "grp"),
            P(None, ("inner", "grp"), "parts"),
        ),
        out_specs=(P(None, ("inner", "grp"), "parts"), P(("parts", "inner"), "grp")),
        check_vma=False,
    )
```
